512 devices in a mesh: dp: 32 (over z_lo, y), tensor: 16 (over z_hi, x, core).
Axes of the slice: x: 4, y: 4, z: 16 (z_hi: 2, z_lo: 8; z = z_hi * 8 + z_lo), core: 2. Of those that a mesh axis runs over, the one named last changes fastest.
Arguments:
- tokens: bfloat16 [16384, 3200], P(('dp', 'tensor')), may hold values from -32 to 32
- norm_gain: bfloat16 [3200], replicated, may hold values from 0.5 to 1.5
- qkv_weight: bfloat16 [3, 3200, 4096], P(None, 'dp', 'tensor'), may hold values from -0.037123106 to 0.037123106
- q_gain: float32 [4096], P('tensor'), may hold values from 1.5 to 5
- k_gain: float32 [4096], P('tensor'), may hold values from 1.5 to 5
- out_weight: bfloat16 [4096, 3200], P('tensor', 'dp'), may hold values from -0.21875 to 0.21875
- layer_scale: float32 [3200], replicated, may hold values from 0.5 to 2
Outputs:
- mixed: bfloat16 [16384, 3200], P(('dp', 'tensor'))
The draws below stay inside these ranges and needn't reach their ends.
All inputs are finite; a program needn't handle non-finite values.
Results may differ from the reference program's by a relative error of at most 0.015.
Values may be sent and summed in bfloat16 or wider, within the bound.
A program may use at most 64 MiB of HBM per device.

```python
import jax
import jax.numpy as jnp
from jax import lax

D = 3200
HEADS = 25
HD = 128
HP = 32
TOK = 512
TOKENS = 16384
N_DP = 32
N_TENSOR = 16


def draw_tokens(key, part):
    key = jax.random.fold_in(key, 11)
    first = jax.random.fold_in(key, 0)
    second = jax.random.fold_in(key, 1)
    fourth = jax.random.fold_in(key, 3)
    base = jnp.clip(jax.random.normal(first, (TOKENS, D), jnp.float32), -4.0, 4.0)
    rows = jnp.exp(jax.random.uniform(second, (TOKENS, 1), jnp.float32, jnp.log(0.5), jnp.log(4.0)))
    cols = jnp.exp(jax.random.uniform(fourth, (1, D), jnp.float32, jnp.log(0.5), jnp.log(2.0)))
    return (base * rows * cols).astype(jnp.bfloat16)


def draw_qkv_weight(key, part):
    key = jax.random.fold_in(key, 12)
    ratio = jnp.minimum((jnp.arange(HP * HD) // HD).astype(jnp.float32) / max(HEADS - 1, 1), 1.0)
    base = jax.random.uniform(key, (3, D, HP * HD), jnp.float32, -1.7, 1.7)
    return (base * jnp.sqrt(0.5 + ratio) * D ** (-0.5)).astype(jnp.bfloat16)


def draw_q_gain(key, part):
    key = jax.random.fold_in(key, 13)
    return jax.random.uniform(key, (HP * HD,), jnp.float32, 1.5, 3.0)


def draw_k_gain(key, part):
    key = jax.random.fold_in(key, 17)
    return jax.random.uniform(key, (HP * HD,), jnp.float32, 1.5, 3.0)


def strengthened(drawn, key, source, target, shards_of, factor):
    owner, partner = [(jnp.arange(drawn.shape[position]) // (drawn.shape[position] // shards_of)).reshape([-1 if axis == position else 1 for axis in range(drawn.ndim)]) for position in (source, target)]
    chosen = jax.random.permutation(key, shards_of)[partner]
    strong = (owner == chosen) | (owner == (partner + shards_of // 2) % shards_of)
    return jnp.where(strong, factor * drawn, drawn)


def levels(rng, dims, cuts, smallest, top_value):
    level, own = 1.0, jax.random.fold_in(rng, 6)
    for position, shards_of in cuts:
        draws = jnp.exp(jax.random.uniform(jax.random.fold_in(own, position), (shards_of,), jnp.float32, smallest / len(cuts), top_value / len(cuts)))
        level = level * jnp.repeat(draws, dims[position] // shards_of).reshape([-1 if axis == position else 1 for axis in range(len(dims))])
    return level


def heavy_noise(rng, dims, scale, most, shards, heavy, held_as=jnp.bfloat16):
    array = scale * jax.random.normal(rng, dims, jnp.float32)
    if shards:
        array = array * levels(rng, dims, shards, -0.22, 0.18)
    return jnp.clip(strengthened(array, jax.random.fold_in(rng, 3), *heavy), -most, most).astype(held_as)


def setup_inputs(seed: int = 0) -> dict:
    streams_of = jax.random.split(jax.random.key(seed), 8)
    return {
        "tokens": draw_tokens(jax.random.fold_in(streams_of[7], 71), 0),
        "norm_gain": jnp.clip(1.0 + 0.1 * jax.random.normal(streams_of[1], (D,), jnp.float32), 0.5, 1.5).astype(jnp.bfloat16),
        "qkv_weight": draw_qkv_weight(jax.random.fold_in(streams_of[7], 71), 0),
        "q_gain": draw_q_gain(jax.random.fold_in(streams_of[7], 71), 0),
        "k_gain": draw_k_gain(jax.random.fold_in(streams_of[7], 71), 0),
        "out_weight": heavy_noise(streams_of[5], (HP * HD, D), (HEADS * HD) ** -0.5, 0.21875, ((0, 16), (1, 32)), (0, 1, 32, 2.75)),
        "layer_scale": jnp.clip(jax.random.uniform(streams_of[6], (D,), jnp.float32, 0.5, 2.0), 0.5, 2.0),
    }


epsilon = 1e-06

def reference(tokens, norm_gain, qkv_weight, q_gain, k_gain, out_weight, layer_scale):
    tiles = tokens.reshape(N_DP, TOK, D)
    scale = HD ** (-0.5)
    keep = (jnp.arange(HP * HD) // HD < HEADS).astype(jnp.float32)
    group_cols = HP * HD // N_TENSOR
    weight_wide = qkv_weight.astype(jnp.float32)
    out_groups = out_weight.astype(jnp.float32).reshape(N_TENSOR, group_cols, D)

    def one_tile(tile):
        row_vals = tile.astype(jnp.float32)
        row_sums = lax.optimization_barrier(jnp.sum(row_vals * row_vals, axis=1, keepdims=True))
        normed = (row_vals * lax.rsqrt(row_sums / D + epsilon) * norm_gain.astype(jnp.float32)).astype(jnp.bfloat16)
        projections = jnp.einsum('td,idc->itc', normed.astype(jnp.float32), weight_wide)
        queries = projections[0] * keep
        keys = projections[1] * keep
        values = projections[2] * keep
        width = HEADS * HD
        query_sums = lax.optimization_barrier(jnp.sum(queries * queries, axis=1, keepdims=True))
        key_sums = lax.optimization_barrier(jnp.sum(keys * keys, axis=1, keepdims=True))
        query_normed = (queries * lax.rsqrt(query_sums / width + epsilon) * q_gain).astype(jnp.bfloat16)
        key_normed = (keys * lax.rsqrt(key_sums / width + epsilon) * k_gain).astype(jnp.bfloat16)
        value_rounded = values.astype(jnp.bfloat16)
        query_heads = query_normed.astype(jnp.float32).reshape(TOK, HP, HD)
        key_heads = key_normed.astype(jnp.float32).reshape(TOK, HP, HD)
        value_heads = value_rounded.astype(jnp.float32).reshape(TOK, HP, HD)
        scores = jnp.einsum('qhd,khd->hqk', query_heads, key_heads) * scale
        probs = jax.nn.softmax(scores, axis=-1).astype(jnp.bfloat16)
        attended = jnp.einsum('hqk,khd->qhd', probs.astype(jnp.float32), value_heads).astype(jnp.bfloat16)
        attended_groups = attended.astype(jnp.float32).reshape(TOK, N_TENSOR, group_cols)
        partials = jnp.einsum('tgc,gcd->gtd', attended_groups, out_groups).astype(jnp.bfloat16)
        projected = lax.optimization_barrier(jnp.sum(partials.astype(jnp.float32), axis=0))
        return (row_vals + layer_scale * projected).astype(jnp.bfloat16)
    return lax.map(one_tile, tiles).reshape(TOKENS, D)
```

```python
import jax
import jax.numpy as jnp
from jax import lax
from jax.experimental import pallas as pl
from jax.experimental.pallas import tpu as pltpu
from jax.sharding import PartitionSpec as P

D = 3200
HEADS = 25
HD = 128
EPS = 1e-06
WIDTH = HEADS * HD
QKV_ROWS = 304
OUT_ROWS = 112
COLS = 640
CHUNKS = D // COLS
MESH = pl.DeviceIdType.MESH
F32 = jnp.float32
BF16 = jnp.bfloat16


def device(y, z, half, x, core):
    return (z * 4 + y, half * 8 + x * 2 + core)


def kernel(
    tok_ref, gain_ref, wa_ref, wb_ref, qg_ref, kg_ref, ls_ref, out_ref,
    xg, abuf, bbuf, wfull, ofull, qkf, heads, att, stage, srecv, szrecv, sown,
    terms, rs1, mid, rs2, wown, wsend, rs3,
    tok_recv, tok_send, w_recv, w_send, s_recv, s_send, r_recv, r_send,
):
    dp = lax.axis_index("dp")
    tensor = lax.axis_index("tensor")
    y, z = dp % 4, dp // 4
    half, x, core = tensor // 8, (tensor // 2) % 4, tensor % 2
    y_up, y_down, y_far = (y + 1) % 4, (y + 3) % 4, (y + 2) % 4
    sibling = device(y, z, half, x, 1 - core)
    across = device(y, z, 1 - half, x, core)

    def near(dx, other):
        c = (core + other) % 2
        return device(y, z, half, (x + dx) % 4, c)

    barrier = pltpu.get_barrier_semaphore()

    def greet(target):
        pl.semaphore_signal(barrier, 1, device_id=target, device_id_type=MESH)

    greet(device(y_up, z, half, x, core))
    greet(device(y_down, z, half, x, core))
    for dx in range(4):
        for other in range(2):
            if dx or other:
                greet(near(dx, other))
    greet(across)

    @pl.when(z > 0)
    def _():
        greet(device(y, z - 1, half, x, core))

    @pl.when(z < 7)
    def _():
        greet(device(y, z + 1, half, x, core))

    def remote(src, dst, send, recv, target):
        return pltpu.make_async_remote_copy(
            src_ref=src, dst_ref=dst, send_sem=send, recv_sem=recv,
            device_id=target, device_id_type=MESH,
        )

    def arrived(ref, sem):
        pltpu.make_async_copy(ref, ref, sem).wait()

    def row_block(h, xx, c):
        return pl.ds(pl.multiple_of(c * 256 + h * 128 + xx * 32, 32), 32)

    tok = tok_ref[...].astype(F32)
    sq = jnp.sum(tok * tok, axis=1, keepdims=True)
    xg[row_block(half, x, core), :] = (
        tok * lax.rsqrt(sq / D + EPS) * gain_ref[...].astype(F32)
    ).astype(BF16)
    mine = z * 4 + y
    abuf[mine] = wa_ref[...]
    bbuf[mine] = wb_ref[...]

    pl.semaphore_wait(
        barrier, 10 + (z > 0).astype(jnp.int32) + (z < 7).astype(jnp.int32)
    )

    def tok_copy(h, xx, c, target, slot):
        ref = xg.at[row_block(h, xx, c), :]
        return remote(
            ref, ref, tok_send.at[slot], tok_recv.at[h * 8 + xx * 2 + c], target
        )

    def tok_wait(h, xx, c):
        arrived(xg.at[row_block(h, xx, c), :], tok_recv.at[h * 8 + xx * 2 + c])

    def tok_spread(h, base):
        for dx in range(1, 4):
            tok_copy(h, x, core, near(dx, 0), base + dx - 1).start()
        tok_copy(h, x, core, sibling, base + 3).start()

    def tok_pass(h, base):
        for dx in range(1, 4):
            xx = (x + dx) % 4
            tok_wait(h, xx, core)
            tok_copy(h, xx, core, sibling, base + dx - 1).start()

    bufs = (abuf, bbuf)

    def z_send(cls, zs, dz, kind):
        b = zs * 4 + y
        ref = bufs[cls].at[b]
        return remote(
            ref, ref, w_send.at[cls, kind, zs], w_recv.at[cls, b, 0],
            device(y, z + dz, half, x, core),
        )

    def y_send(cls, zs, yt, kind):
        b = zs * 4 + y
        ref = bufs[cls].at[b]
        return remote(
            ref, ref, w_send.at[cls, kind, zs], w_recv.at[cls, b, 0],
            device(yt, z, half, x, core),
        )

    def y_pass(cls, zs, ysrc, yt, part, kind):
        b = zs * 4 + ysrc
        ref = bufs[cls].at[b, :, pl.ds(part * 128, 128)]
        return remote(
            ref, ref, w_send.at[cls, kind, zs], w_recv.at[cls, b, part],
            device(yt, z, half, x, core),
        )

    def send_y(cls, zs):
        y_send(cls, zs, y_up, 2).start()
        y_send(cls, zs, y_down, 3).start()

    def first_step(cls):
        @pl.when(z < 7)
        def _():
            z_send(cls, z, 1, 0).start()

        @pl.when(z > 0)
        def _():
            z_send(cls, z, -1, 1).start()

        send_y(cls, z)

    def step(cls, s):
        @pl.when(z >= s)
        def _():
            zs = z - s
            arrived(bufs[cls].at[zs * 4 + y], w_recv.at[cls, zs * 4 + y, 0])

            @pl.when(z < 7)
            def _():
                z_send(cls, zs, 1, 0).start()

            send_y(cls, zs)

        @pl.when(z + s <= 7)
        def _():
            zs = z + s
            arrived(bufs[cls].at[zs * 4 + y], w_recv.at[cls, zs * 4 + y, 0])

            @pl.when(z > 0)
            def _():
                z_send(cls, zs, -1, 1).start()

            send_y(cls, zs)

    def pass_one(cls, zs):
        arrived(bufs[cls].at[zs * 4 + y_down], w_recv.at[cls, zs * 4 + y_down, 0])
        y_pass(cls, zs, y_down, y_up, 0, 4).start()
        arrived(bufs[cls].at[zs * 4 + y_up], w_recv.at[cls, zs * 4 + y_up, 0])
        y_pass(cls, zs, y_up, y_down, 1, 5).start()

    def passes(cls, s):
        @pl.when(z >= s)
        def _():
            pass_one(cls, z - s)

        @pl.when((z + s <= 7) & (s > 0))
        def _():
            pass_one(cls, z + s)

    def finish(cls, zs):
        b = zs * 4 + y_far
        for part in range(2):
            arrived(
                bufs[cls].at[b, :, pl.ds(part * 128, 128)], w_recv.at[cls, b, part]
            )

    def sent(cls):
        @pl.loop(0, 8)
        def _(zs):
            @pl.when((z < 7) & (zs <= z))
            def _():
                z_send(cls, zs, 1, 0).wait_send()

            @pl.when((z > 0) & (zs >= z))
            def _():
                z_send(cls, zs, -1, 1).wait_send()

            y_send(cls, zs, y_up, 2).wait_send()
            y_send(cls, zs, y_down, 3).wait_send()
            y_pass(cls, zs, y_down, y_up, 0, 4).wait_send()
            y_pass(cls, zs, y_up, y_down, 1, 5).wait_send()

    tok_copy(half, x, core, across, 0).start()
    tok_spread(half, 1)
    first_step(0)

    @pl.loop(1, 4)
    def _(s):
        step(0, s)
        passes(0, s - 1)

    tok_pass(half, 5)

    @pl.loop(4, 8)
    def _(s):
        step(0, s)
        passes(0, s - 1)

    passes(0, 7)
    tok_wait(1 - half, x, core)
    tok_spread(1 - half, 8)
    first_step(1)

    @pl.loop(1, 8)
    def _(s):
        step(1, s)

    tok_pass(1 - half, 12)

    @pl.loop(0, 8)
    def _(zs):
        finish(0, zs)
        rows = pl.ds(pl.multiple_of(zs * 400, 16), 400)
        for i in range(3):
            wfull[i, rows, :] = jnp.concatenate(
                [abuf[zs * 4 + j, i * 100 : i * 100 + 100, :] for j in range(4)], axis=0
            )

    for h in range(2):
        for xx in range(4):
            tok_wait(h, xx, 1 - core)

    keep = (
        tensor * 2 + lax.broadcasted_iota(jnp.int32, (1, 256), 1) // HD < HEADS
    ).astype(F32)

    def project(i):
        return jnp.dot(xg[...], wfull[i], preferred_element_type=F32) * keep

    sums = []
    for i in range(2):
        qkf[i] = project(i)
        sums.append(jnp.sum(qkf[i] * qkf[i], axis=1, keepdims=True))
    lane = lax.broadcasted_iota(jnp.int32, (512, 128), 1)
    stage[...] = jnp.where(
        lane == 0, sums[0], jnp.where(lane == 1, sums[1], 0.0)
    ).T
    spot = x * 2 + core
    for i in range(2):
        for j in range(4):
            srecv[spot, pl.ds(i * 4 + j, 1), :] = stage[i : i + 1, j * 128 : j * 128 + 128]

    def sum_copy(dx, other):
        return remote(
            srecv.at[spot], srecv.at[spot], s_send.at[dx * 2 + other],
            s_recv.at[spot], near(dx, other),
        )

    for dx in range(4):
        for other in range(2):
            if dx or other:
                sum_copy(dx, other).start()

    heads[2] = project(2).astype(BF16)

    @pl.loop(0, 8)
    def _(s):
        passes(1, s)

    for dx in range(4):
        for other in range(2):
            if dx or other:
                other_spot = ((x + dx) % 4) * 2 + (core + other) % 2
                arrived(srecv.at[other_spot], s_recv.at[other_spot])
    total = srecv[0]
    for i in range(1, 8):
        total += srecv[i]
    sown[...] = total
    across_sum = remote(sown, szrecv, s_send.at[0], s_recv.at[8], across)
    for dx in range(4):
        for other in range(2):
            if dx or other:
                sum_copy(dx, other).wait_send()
    across_sum.start()

    @pl.loop(0, 8)
    def _(zs):
        finish(1, zs)
        ofull[pl.ds(pl.multiple_of(zs * 400, 16), 400), :] = jnp.concatenate(
            [bbuf[zs * 4 + j, 0:100, :] for j in range(4)], axis=0
        )

    across_sum.wait()
    total = sown[...] + szrecv[...]
    for i in range(2):
        for j in range(4):
            stage[i : i + 1, j * 128 : j * 128 + 128] = total[i * 4 + j : i * 4 + j + 1, :]
    columns = stage[...].T
    heads[0] = (
        qkf[0] * lax.rsqrt(columns[:, 0:1] / WIDTH + EPS) * qg_ref[...]
    ).astype(BF16)
    heads[1] = (
        qkf[1] * lax.rsqrt(columns[:, 1:2] / WIDTH + EPS) * kg_ref[...]
    ).astype(BF16)

    for h in range(2):
        cols = slice(h * HD, h * HD + HD)

        @pl.loop(0, 2)
        def _(r):
            rows = pl.ds(pl.multiple_of(r * 256, 256), 256)
            scores = lax.dot_general(
                heads[0, rows, cols], heads[1, :, cols], (((1,), (1,)), ((), ())),
                preferred_element_type=F32,
            ) * HD ** (-0.5)
            e = jnp.exp(scores - jnp.max(scores, axis=1, keepdims=True))
            probs = (e / jnp.sum(e, axis=1, keepdims=True)).astype(BF16)
            att[rows, cols] = jnp.dot(
                probs, heads[2, :, cols], preferred_element_type=F32
            ).astype(BF16)

    def to_sibling(c):
        return remote(
            terms.at[c, 1 - core], rs1.at[c], r_send.at[c, 0], r_recv.at[c, 0], sibling
        )

    def to_near(c, dx):
        return remote(
            mid.at[c, (x + dx) % 4], rs2.at[c, dx - 1], r_send.at[c, dx],
            r_recv.at[c, dx], near(dx, 0),
        )

    def to_across(c):
        return remote(wsend.at[c], rs3.at[c], r_send.at[c, 4], r_recv.at[c, 4], across)

    def stage_one(c):
        part = lax.dot_general(
            att[...], ofull[c * COLS : c * COLS + COLS, :], (((1,), (1,)), ((), ())),
            preferred_element_type=F32,
        )
        terms[c] = part.astype(BF16).reshape(2, 256, COLS)
        to_sibling(c).start()

    def stage_two(c):
        arrived(rs1.at[c], r_recv.at[c, 0])
        both = (terms[c, core].astype(F32) + rs1[c].astype(F32)).astype(BF16)
        both = both.reshape(2, 4, 32, COLS)
        for xx in range(4):
            for h in range(2):
                mid[c, xx, h] = both[h, xx]
        for dx in range(1, 4):
            to_near(c, dx).start()

    def stage_three(c):
        for dx in range(1, 4):
            arrived(rs2.at[c, dx - 1], r_recv.at[c, dx])

        def summed(h):
            s = mid[c, x, h].astype(F32)
            for dx in range(3):
                s += rs2[c, dx, h].astype(F32)
            return s

        wsend[c] = summed(1 - half).astype(BF16)
        to_across(c).start()
        wown[c] = summed(half)

    def stage_four(c):
        arrived(rs3.at[c], r_recv.at[c, 4])
        cols = slice(c * COLS, c * COLS + COLS)
        projected = wown[c] + rs3[c].astype(F32)
        out_ref[:, cols] = (
            tok_ref[:, cols].astype(F32) + ls_ref[:, cols] * projected
        ).astype(BF16)

    for t in range(CHUNKS + 3):
        if t < CHUNKS:
            stage_one(t)
        if 0 <= t - 1 < CHUNKS:
            stage_two(t - 1)
        if 0 <= t - 2 < CHUNKS:
            stage_three(t - 2)
    for c in range(CHUNKS):
        stage_four(c)

    for slot in range(15):
        tok_copy(half, x, core, sibling, slot).wait_send()
    sent(0)
    sent(1)
    for c in range(CHUNKS):
        to_sibling(c).wait_send()
        for dx in range(1, 4):
            to_near(c, dx).wait_send()
        to_across(c).wait_send()


def shards(tokens, norm_gain, qkv_weight, q_gain, k_gain, out_weight, layer_scale):
    wa = jnp.pad(qkv_weight.reshape(300, 256), ((0, QKV_ROWS - 300), (0, 0)))
    wb = jnp.pad(out_weight.T, ((0, OUT_ROWS - 100), (0, 0)))
    vmem = pl.BlockSpec(memory_space=pltpu.VMEM)
    dma = pltpu.SemaphoreType.DMA
    return pl.pallas_call(
        kernel,
        out_shape=jax.ShapeDtypeStruct((32, D), BF16),
        in_specs=[vmem] * 7,
        out_specs=vmem,
        scratch_shapes=[
            pltpu.VMEM((512, D), BF16),
            pltpu.VMEM((32, QKV_ROWS, 256), BF16),
            pltpu.VMEM((32, OUT_ROWS, 256), BF16),
            pltpu.VMEM((3, D, 256), BF16),
            pltpu.VMEM((D, 256), BF16),
            pltpu.VMEM((2, 512, 256), F32),
            pltpu.VMEM((3, 512, 256), BF16),
            pltpu.VMEM((512, 256), BF16),
            pltpu.VMEM((128, 512), F32),
            pltpu.VMEM((8, 8, 128), F32),
            pltpu.VMEM((8, 128), F32),
            pltpu.VMEM((8, 128), F32),
            pltpu.VMEM((CHUNKS, 2, 256, COLS), BF16),
            pltpu.VMEM((CHUNKS, 256, COLS), BF16),
            pltpu.VMEM((CHUNKS, 4, 2, 32, COLS), BF16),
            pltpu.VMEM((CHUNKS, 3, 2, 32, COLS), BF16),
            pltpu.VMEM((CHUNKS, 32, COLS), F32),
            pltpu.VMEM((CHUNKS, 32, COLS), BF16),
            pltpu.VMEM((CHUNKS, 32, COLS), BF16),
            dma((16,)),
            dma((15,)),
            dma((2, 32, 2)),
            dma((2, 6, 8)),
            dma((9,)),
            dma((8,)),
            dma((CHUNKS, 5)),
            dma((CHUNKS, 5)),
        ],
        compiler_params=pltpu.CompilerParams(
            collective_id=0, has_side_effects=True, vmem_limit_bytes=60 * 1024 * 1024
        ),
        cost_estimate=pl.CostEstimate(
            flops=4_000_000_000, bytes_accessed=1_000_000, transcendentals=600_000
        ),
    )(
        tokens, norm_gain.reshape(1, D), wa, wb, q_gain.reshape(1, 256),
        k_gain.reshape(1, 256), layer_scale.reshape(1, D),
    )


def solution(mesh):
    placed = (
        P(("dp", "tensor"), None),
        P(),
        P(None, "dp", "tensor"),
        P("tensor"),
        P("tensor"),
        P("tensor", "dp"),
        P(),
    )
    return jax.shard_map(
        shards, mesh=mesh, in_specs=placed, out_specs=P(("dp", "tensor"), None), check_vma=False
    )
```

```python
import jax
import jax.numpy as jnp
from jax import lax
from jax.experimental import pallas as pl
from jax.experimental.pallas import tpu as pltpu
from jax.sharding import PartitionSpec as P

D = 3200
HEADS = 25
HD = 128
EPS = 1e-06
WIDTH = HEADS * HD
QKV_ROWS = 304
OUT_ROWS = 112
COLS = 640
CHUNKS = D // COLS
MESH = pl.DeviceIdType.MESH
F32 = jnp.float32
BF16 = jnp.bfloat16


def device(y, z, half, x, core):
    return (z * 4 + y, half * 8 + x * 2 + core)


def kernel(
    tok_ref, gain_ref, qkv_ref, o_ref, qg_ref, kg_ref, ls_ref, out_ref,
    xg, abuf, bbuf, wfull, ofull, qkf, heads, att, stage, srecv, szrecv, sown,
    terms, rs1, mid, rs2, wown, wsend, rs3,
    tok_recv, tok_send, w_recv, w_send, s_recv, s_send, r_recv, r_send,
):
    dp = lax.axis_index("dp")
    tensor = lax.axis_index("tensor")
    y, z = dp % 4, dp // 4
    half, x, core = tensor // 8, (tensor // 2) % 4, tensor % 2
    y_up, y_down, y_far = (y + 1) % 4, (y + 3) % 4, (y + 2) % 4
    sibling = device(y, z, half, x, 1 - core)
    across = device(y, z, 1 - half, x, core)

    def near(dx, other):
        c = (core + other) % 2
        return device(y, z, half, (x + dx) % 4, c)

    barrier = pltpu.get_barrier_semaphore()

    def greet(target):
        pl.semaphore_signal(barrier, 1, device_id=target, device_id_type=MESH)

    greet(across)
    greet(device(y_up, z, half, x, core))
    greet(device(y_down, z, half, x, core))
    for dx in range(4):
        for other in range(2):
            if dx or other:
                greet(near(dx, other))

    @pl.when(z > 0)
    def _():
        greet(device(y, z - 1, half, x, core))

    @pl.when(z < 7)
    def _():
        greet(device(y, z + 1, half, x, core))

    def remote(src, dst, send, recv, target):
        return pltpu.make_async_remote_copy(
            src_ref=src, dst_ref=dst, send_sem=send, recv_sem=recv,
            device_id=target, device_id_type=MESH,
        )

    def arrived(ref, sem):
        pltpu.make_async_copy(ref, ref, sem).wait()

    def row_block(h, xx, c, p):
        return pl.ds(pl.multiple_of(c * 256 + h * 128 + xx * 32 + p * 16, 16), 16)

    tok = tok_ref[...].astype(F32)
    sq = jnp.sum(tok * tok, axis=1, keepdims=True)
    normed = (
        tok * lax.rsqrt(sq / D + EPS) * gain_ref[...].astype(F32).reshape(1, D)
    ).astype(BF16)
    for p in range(2):
        xg[row_block(half, x, core, p), :] = normed[p * 16 : p * 16 + 16, :]
    mine = z * 4 + y
    for p in range(2):
        cols = slice(p * 128, p * 128 + 128)
        abuf[mine, p] = jnp.concatenate(
            [qkv_ref[i, :, cols] for i in range(3)]
            + [jnp.zeros((QKV_ROWS - 300, 128), BF16)],
            axis=0,
        )
    for p in range(2):
        bbuf[mine, p] = jnp.concatenate(
            [
                o_ref[:, p * 128 : p * 128 + 128],
                jnp.zeros((OUT_ROWS - 100, 128), BF16),
            ],
            axis=0,
        )

    pl.semaphore_wait(
        barrier, 10 + (z > 0).astype(jnp.int32) + (z < 7).astype(jnp.int32)
    )

    def tok_copy(h, xx, c, p, target, slot):
        ref = xg.at[row_block(h, xx, c, p), :]
        return remote(
            ref, ref, tok_send.at[slot, p], tok_recv.at[h * 8 + xx * 2 + c, p], target
        )

    def tok_wait(h, xx, c, p):
        arrived(xg.at[row_block(h, xx, c, p), :], tok_recv.at[h * 8 + xx * 2 + c, p])

    def tok_spread(h, p, base):
        for dx in (2, 1, 3):
            tok_copy(h, x, core, p, near(dx, 0), base + dx - 1).start()
        tok_copy(h, x, core, p, sibling, base + 3).start()

    def tok_pass(h, p, base):
        for dx in (1, 3, 2):
            xx = (x + dx) % 4
            tok_wait(h, xx, core, p)
            tok_copy(h, xx, core, p, sibling, base + dx - 1).start()

    bufs = (abuf, bbuf)

    def w_copy(cls, zs, yy, part, kind, target):
        b = zs * 4 + yy
        ref = bufs[cls].at[b, part]
        return remote(
            ref, ref, w_send.at[cls, kind, zs, part], w_recv.at[cls, b, part], target
        )

    def w_wait(cls, zs, yy, part):
        b = zs * 4 + yy
        arrived(bufs[cls].at[b, part], w_recv.at[cls, b, part])

    def z_right(cls, zs, part):
        return w_copy(cls, zs, y, part, 0, device(y, z + 1, half, x, core))

    def z_left(cls, zs, part):
        return w_copy(cls, zs, y, part, 1, device(y, z - 1, half, x, core))

    def y_plus(cls, zs, part):
        return w_copy(cls, zs, y, part, 2, device(y_up, z, half, x, core))

    def y_minus(cls, zs, part):
        return w_copy(cls, zs, y, part, 3, device(y_down, z, half, x, core))

    def pass_plus(cls, zs):
        return w_copy(cls, zs, y_down, 0, 4, device(y_up, z, half, x, core))

    def pass_minus(cls, zs):
        return w_copy(cls, zs, y_up, 1, 5, device(y_down, z, half, x, core))

    def send_y(cls, zs):
        y_plus(cls, zs, 0).start()
        y_minus(cls, zs, 1).start()
        y_plus(cls, zs, 1).start()
        y_minus(cls, zs, 0).start()

    def first_step(cls, spread):
        for part in range(2):

            @pl.when(z < 7)
            def _():
                z_right(cls, z, part).start()

            @pl.when(z > 0)
            def _():
                z_left(cls, z, part).start()

        if spread:
            send_y(cls, z)

    def step(cls, s, spread):
        for part in range(2):

            @pl.when(z >= s)
            def _():
                w_wait(cls, z - s, y, part)

                @pl.when(z < 7)
                def _():
                    z_right(cls, z - s, part).start()

            @pl.when(z + s <= 7)
            def _():
                w_wait(cls, z + s, y, part)

                @pl.when(z > 0)
                def _():
                    z_left(cls, z + s, part).start()

        if spread:

            @pl.when(z >= s)
            def _():
                send_y(cls, z - s)

            @pl.when(z + s <= 7)
            def _():
                send_y(cls, z + s)

    def pass_one(cls, zs):
        w_wait(cls, zs, y_down, 0)
        pass_plus(cls, zs).start()
        w_wait(cls, zs, y_up, 1)
        pass_minus(cls, zs).start()

    def passes(cls, s):
        @pl.when(z >= s)
        def _():
            pass_one(cls, z - s)

        @pl.when((z + s <= 7) & (s > 0))
        def _():
            pass_one(cls, z + s)

    def finish(cls, zs):
        w_wait(cls, zs, y_down, 1)
        w_wait(cls, zs, y_up, 0)
        for part in range(2):
            w_wait(cls, zs, y_far, part)

    def sent(cls):
        @pl.loop(0, 8)
        def _(zs):
            for part in range(2):

                @pl.when((z < 7) & (zs <= z))
                def _():
                    z_right(cls, zs, part).wait_send()

                @pl.when((z > 0) & (zs >= z))
                def _():
                    z_left(cls, zs, part).wait_send()

                y_plus(cls, zs, part).wait_send()
                y_minus(cls, zs, part).wait_send()
            pass_plus(cls, zs).wait_send()
            pass_minus(cls, zs).wait_send()

    for p in range(2):
        tok_copy(half, x, core, p, across, 0).start()
    first_step(0, True)
    for p in range(2):
        tok_spread(half, p, 1)

    @pl.loop(1, 3)
    def _(s):
        step(0, s, True)

    step(0, 3, True)
    passes(0, 0)
    for p in range(2):
        tok_pass(half, p, 5)
    tok_wait(1 - half, x, core, 0)
    tok_spread(1 - half, 0, 8)
    step(0, 4, True)
    passes(0, 1)
    tok_wait(1 - half, x, core, 1)
    tok_spread(1 - half, 1, 8)
    first_step(1, False)

    @pl.loop(5, 8)
    def _(s):
        step(0, s, True)
        passes(0, s - 3)
        step(1, s - 4, False)

    for p in range(2):
        tok_pass(1 - half, p, 12)

    @pl.loop(5, 8)
    def _(s):
        passes(0, s)
        step(1, s - 1, False)

    step(1, 7, False)

    @pl.loop(0, 8)
    def _(s):
        @pl.when(z >= s)
        def _():
            send_y(1, z - s)

        @pl.when((z + s <= 7) & (s > 0))
        def _():
            send_y(1, z + s)

    @pl.loop(0, 8)
    def _(zs):
        finish(0, zs)
        rows = pl.ds(pl.multiple_of(zs * 400, 16), 400)
        for i in range(3):
            for p in range(2):
                wfull[i, rows, p * 128 : p * 128 + 128] = jnp.concatenate(
                    [abuf[zs * 4 + j, p, i * 100 : i * 100 + 100, :] for j in range(4)],
                    axis=0,
                )

    for h in range(2):
        for xx in range(4):
            for p in range(2):
                tok_wait(h, xx, 1 - core, p)

    keep = (
        tensor * 2 + lax.broadcasted_iota(jnp.int32, (1, 256), 1) // HD < HEADS
    ).astype(F32)

    def project(i):
        return jnp.dot(xg[...], wfull[i], preferred_element_type=F32) * keep

    sums = []
    for i in range(2):
        qkf[i] = project(i)
        sums.append(jnp.sum(qkf[i] * qkf[i], axis=1, keepdims=True))
    lane = lax.broadcasted_iota(jnp.int32, (512, 128), 1)
    stage[...] = jnp.where(
        lane == 0, sums[0], jnp.where(lane == 1, sums[1], 0.0)
    ).T
    spot = x * 2 + core
    for i in range(2):
        for j in range(4):
            srecv[spot, pl.ds(i * 4 + j, 1), :] = stage[i : i + 1, j * 128 : j * 128 + 128]

    def sum_copy(dx, other):
        return remote(
            srecv.at[spot], srecv.at[spot], s_send.at[dx * 2 + other],
            s_recv.at[spot], near(dx, other),
        )

    for dx in range(4):
        for other in range(2):
            if dx or other:
                sum_copy(dx, other).start()

    heads[2] = project(2).astype(BF16)

    @pl.loop(0, 4)
    def _(s):
        passes(1, s)

    for dx in range(4):
        for other in range(2):
            if dx or other:
                other_spot = ((x + dx) % 4) * 2 + (core + other) % 2
                arrived(srecv.at[other_spot], s_recv.at[other_spot])
    total = srecv[0]
    for i in range(1, 8):
        total += srecv[i]
    sown[...] = total
    across_sum = remote(sown, szrecv, s_send.at[0], s_recv.at[8], across)
    for dx in range(4):
        for other in range(2):
            if dx or other:
                sum_copy(dx, other).wait_send()
    across_sum.start()

    @pl.loop(4, 8)
    def _(s):
        passes(1, s)

    across_sum.wait()
    total = sown[...] + szrecv[...]
    for i in range(2):
        for j in range(4):
            stage[i : i + 1, j * 128 : j * 128 + 128] = total[i * 4 + j : i * 4 + j + 1, :]
    columns = stage[...].T
    heads[0] = (
        qkf[0] * lax.rsqrt(columns[:, 0:1] / WIDTH + EPS) * qg_ref[...].reshape(1, 256)
    ).astype(BF16)
    heads[1] = (
        qkf[1] * lax.rsqrt(columns[:, 1:2] / WIDTH + EPS) * kg_ref[...].reshape(1, 256)
    ).astype(BF16)

    for h in range(2):
        cols = slice(h * HD, h * HD + HD)

        @pl.loop(0, 2)
        def _(r):
            rows = pl.ds(pl.multiple_of(r * 256, 256), 256)
            scores = lax.dot_general(
                heads[0, rows, cols], heads[1, :, cols], (((1,), (1,)), ((), ())),
                preferred_element_type=F32,
            ) * HD ** (-0.5)
            e = jnp.exp(scores - jnp.max(scores, axis=1, keepdims=True))
            probs = (e / jnp.sum(e, axis=1, keepdims=True)).astype(BF16)
            att[rows, cols] = jnp.dot(
                probs, heads[2, :, cols], preferred_element_type=F32
            ).astype(BF16)

    for slot in range(15):
        for p in range(2):
            tok_copy(half, x, core, p, sibling, slot).wait_send()
    sent(0)

    @pl.loop(0, 8)
    def _(zs):
        finish(1, zs)
        rows = pl.ds(pl.multiple_of(zs * 400, 16), 400)
        for p in range(2):
            ofull[rows, p * 128 : p * 128 + 128] = jnp.concatenate(
                [bbuf[zs * 4 + j, p, 0:100, :] for j in range(4)], axis=0
            )

    def to_sibling(c):
        return remote(
            terms.at[c, 1 - core], rs1.at[c], r_send.at[c, 0], r_recv.at[c, 0], sibling
        )

    def to_near(c, dx):
        return remote(
            mid.at[c, (x + dx) % 4], rs2.at[c, dx - 1], r_send.at[c, dx],
            r_recv.at[c, dx], near(dx, 0),
        )

    def to_across(c):
        return remote(wsend.at[c], rs3.at[c], r_send.at[c, 4], r_recv.at[c, 4], across)

    def stage_one(c):
        part = lax.dot_general(
            att[...], ofull[c * COLS : c * COLS + COLS, :], (((1,), (1,)), ((), ())),
            preferred_element_type=F32,
        )
        terms[c] = part.astype(BF16).reshape(2, 256, COLS)
        to_sibling(c).start()

    def stage_two(c):
        arrived(rs1.at[c], r_recv.at[c, 0])
        both = (terms[c, core].astype(F32) + rs1[c].astype(F32)).astype(BF16)
        both = both.reshape(2, 4, 32, COLS)
        for xx in range(4):
            for h in range(2):
                mid[c, xx, h] = both[h, xx]
        for dx in range(1, 4):
            to_near(c, dx).start()

    def stage_three(c):
        for dx in range(1, 4):
            arrived(rs2.at[c, dx - 1], r_recv.at[c, dx])

        def summed(h):
            s = mid[c, x, h].astype(F32)
            for dx in range(3):
                s += rs2[c, dx, h].astype(F32)
            return s

        wsend[c] = summed(1 - half).astype(BF16)
        to_across(c).start()
        wown[c] = summed(half)

    scale = ls_ref[...].reshape(1, D)

    def stage_four(c):
        arrived(rs3.at[c], r_recv.at[c, 4])
        cols = slice(c * COLS, c * COLS + COLS)
        projected = wown[c] + rs3[c].astype(F32)
        out_ref[:, cols] = (
            tok_ref[:, cols].astype(F32) + scale[:, cols] * projected
        ).astype(BF16)

    for t in range(CHUNKS + 3):
        if t < CHUNKS:
            stage_one(t)
        if 0 <= t - 1 < CHUNKS:
            stage_two(t - 1)
        if 0 <= t - 2 < CHUNKS:
            stage_three(t - 2)
    for c in range(CHUNKS):
        stage_four(c)

    sent(1)
    for c in range(CHUNKS):
        to_sibling(c).wait_send()
        for dx in range(1, 4):
            to_near(c, dx).wait_send()
        to_across(c).wait_send()


def shards(tokens, norm_gain, qkv_weight, q_gain, k_gain, out_weight, layer_scale):
    vmem = pl.BlockSpec(memory_space=pltpu.VMEM)
    dma = pltpu.SemaphoreType.DMA
    return pl.pallas_call(
        kernel,
        out_shape=jax.ShapeDtypeStruct((32, D), BF16),
        in_specs=[vmem] * 7,
        out_specs=vmem,
        scratch_shapes=[
            pltpu.VMEM((512, D), BF16),
            pltpu.VMEM((32, 2, QKV_ROWS, 128), BF16),
            pltpu.VMEM((32, 2, OUT_ROWS, 128), BF16),
            pltpu.VMEM((3, D, 256), BF16),
            pltpu.VMEM((D, 256), BF16),
            pltpu.VMEM((2, 512, 256), F32),
            pltpu.VMEM((3, 512, 256), BF16),
            pltpu.VMEM((512, 256), BF16),
            pltpu.VMEM((128, 512), F32),
            pltpu.VMEM((8, 8, 128), F32),
            pltpu.VMEM((8, 128), F32),
            pltpu.VMEM((8, 128), F32),
            pltpu.VMEM((CHUNKS, 2, 256, COLS), BF16),
            pltpu.VMEM((CHUNKS, 256, COLS), BF16),
            pltpu.VMEM((CHUNKS, 4, 2, 32, COLS), BF16),
            pltpu.VMEM((CHUNKS, 3, 2, 32, COLS), BF16),
            pltpu.VMEM((CHUNKS, 32, COLS), F32),
            pltpu.VMEM((CHUNKS, 32, COLS), BF16),
            pltpu.VMEM((CHUNKS, 32, COLS), BF16),
            dma((16, 2)),
            dma((15, 2)),
            dma((2, 32, 2)),
            dma((2, 6, 8, 2)),
            dma((9,)),
            dma((8,)),
            dma((CHUNKS, 5)),
            dma((CHUNKS, 5)),
        ],
        compiler_params=pltpu.CompilerParams(
            collective_id=0, has_side_effects=True, vmem_limit_bytes=60 * 1024 * 1024
        ),
        cost_estimate=pl.CostEstimate(
            flops=4_000_000_000, bytes_accessed=1_000_000, transcendentals=600_000
        ),
    )(
        tokens, norm_gain, qkv_weight, out_weight.T, q_gain, k_gain, layer_scale
    )


def solution(mesh):
    placed = (
        P(("dp", "tensor"), None),
        P(),
        P(None, "dp", "tensor"),
        P("tensor"),
        P("tensor"),
        P("tensor", "dp"),
        P(),
    )
    return jax.shard_map(
        shards, mesh=mesh, in_specs=placed, out_specs=P(("dp", "tensor"), None), check_vma=False
    )
```

```python
import jax
import jax.numpy as jnp
from jax import lax
from jax.experimental import pallas as pl
from jax.experimental.pallas import tpu as pltpu
from jax.sharding import PartitionSpec as P

D = 3200
HEADS = 25
HD = 128
EPS = 1e-06
WIDTH = HEADS * HD
QKV_ROWS = 304
OUT_ROWS = 112
COLS = (256, 512, 512, 640, 512, 512, 256)
CHUNKS = len(COLS)
STARTS = tuple(sum(COLS[:c]) for c in range(CHUNKS))
MESH = pl.DeviceIdType.MESH
F32 = jnp.float32
BF16 = jnp.bfloat16


def device(y, z, half, x, core):
    return (z * 4 + y, half * 8 + x * 2 + core)


def kernel(*refs):
    tok_ref, gain_ref, qkv_ref, o_ref, qg_ref, kg_ref, ls_ref, out_ref = refs[:8]
    xg, abuf, bbuf, wfull, ofull, qkf, heads, att, stage, srecv, szrecv, sown = refs[8:20]
    chunk_refs = refs[20:-10]
    terms, rs1, mid, far, added, rs2, wown, wsend, rs3 = [
        chunk_refs[i * CHUNKS : (i + 1) * CHUNKS] for i in range(9)
    ]
    tok_recv, tok_send, z8_recv, z8_send, w_recv, w_send = refs[-10:-4]
    s_recv, s_send, r_recv, r_send = refs[-4:]
    dp = lax.axis_index("dp")
    tensor = lax.axis_index("tensor")
    y, z = dp % 4, dp // 4
    half, x, core = tensor // 8, (tensor // 2) % 4, tensor % 2
    y_up, y_down, y_far = (y + 1) % 4, (y + 3) % 4, (y + 2) % 4
    sibling = device(y, z, half, x, 1 - core)
    across = device(y, z, 1 - half, x, core)

    def near(dx, other):
        c = (core + other) % 2
        return device(y, z, half, (x + dx) % 4, c)

    barrier = pltpu.get_barrier_semaphore()

    def greet(target):
        pl.semaphore_signal(barrier, 1, device_id=target, device_id_type=MESH)

    greet(across)
    greet(device(y_up, z, half, x, core))
    greet(device(y_down, z, half, x, core))
    for dx in range(4):
        for other in range(2):
            if dx or other:
                greet(near(dx, other))

    @pl.when(z > 0)
    def _():
        greet(device(y, z - 1, half, x, core))

    @pl.when(z < 7)
    def _():
        greet(device(y, z + 1, half, x, core))

    def remote(src, dst, send, recv, target):
        return pltpu.make_async_remote_copy(
            src_ref=src, dst_ref=dst, send_sem=send, recv_sem=recv,
            device_id=target, device_id_type=MESH,
        )

    def arrived(ref, sem):
        pltpu.make_async_copy(ref, ref, sem).wait()

    def row_block(h, xx, c, p):
        return pl.ds(pl.multiple_of(c * 256 + h * 128 + xx * 32 + p * 16, 16), 16)

    tok = tok_ref[...].astype(F32)
    sq = jnp.sum(tok * tok, axis=1, keepdims=True)
    normed = (
        tok * lax.rsqrt(sq / D + EPS) * gain_ref[...].astype(F32).reshape(1, D)
    ).astype(BF16)
    for p in range(2):
        xg[row_block(half, x, core, p), :] = normed[p * 16 : p * 16 + 16, :]
    mine = z * 4 + y
    for p in range(2):
        cols = slice(p * 128, p * 128 + 128)
        abuf[mine, p] = jnp.concatenate(
            [qkv_ref[i, :, cols] for i in range(3)]
            + [jnp.zeros((QKV_ROWS - 300, 128), BF16)],
            axis=0,
        )
    for p in range(2):
        bbuf[mine, p] = jnp.concatenate(
            [
                o_ref[:, p * 128 : p * 128 + 128],
                jnp.zeros((OUT_ROWS - 100, 128), BF16),
            ],
            axis=0,
        )

    pl.semaphore_wait(
        barrier, 10 + (z > 0).astype(jnp.int32) + (z < 7).astype(jnp.int32)
    )

    def tok_copy(h, xx, c, p, target, slot):
        ref = xg.at[row_block(h, xx, c, p), :]
        return remote(
            ref, ref, tok_send.at[slot, p], tok_recv.at[h * 8 + xx * 2 + c, p], target
        )

    def tok_wait(h, xx, c, p):
        arrived(xg.at[row_block(h, xx, c, p), :], tok_recv.at[h * 8 + xx * 2 + c, p])

    def tok_spread(h, p, base):
        for dx in (2, 1, 3):
            tok_copy(h, x, core, p, near(dx, 0), base + dx - 1).start()
        tok_copy(h, x, core, p, sibling, base + 3).start()

    def tok_pass(h, p, base):
        for dx in (1, 3, 2):
            xx = (x + dx) % 4
            tok_wait(h, xx, core, p)
            tok_copy(h, xx, core, p, sibling, base + dx - 1).start()


    def z8_copy(k):
        ref = xg.at[pl.ds(pl.multiple_of(core * 256 + half * 128 + x * 32, 32), 32), pl.ds(k * 640, 640)]
        return remote(ref, ref, z8_send.at[k], z8_recv.at[k], across)

    def z8_wait(k):
        ref = xg.at[pl.ds(pl.multiple_of(core * 256 + (1 - half) * 128 + x * 32, 32), 32), pl.ds(k * 640, 640)]
        arrived(ref, z8_recv.at[k])

    bufs = (abuf, bbuf)

    def w_copy(cls, zs, yy, part, kind, target):
        b = zs * 4 + yy
        ref = bufs[cls].at[b, part]
        return remote(
            ref, ref, w_send.at[cls, kind, zs, part], w_recv.at[cls, b, part], target
        )

    def w_wait(cls, zs, yy, part):
        b = zs * 4 + yy
        arrived(bufs[cls].at[b, part], w_recv.at[cls, b, part])

    def z_right(cls, zs, part):
        return w_copy(cls, zs, y, part, 0, device(y, z + 1, half, x, core))

    def z_left(cls, zs, part):
        return w_copy(cls, zs, y, part, 1, device(y, z - 1, half, x, core))

    def y_plus(cls, zs, part):
        return w_copy(cls, zs, y, part, 2, device(y_up, z, half, x, core))

    def y_minus(cls, zs, part):
        return w_copy(cls, zs, y, part, 3, device(y_down, z, half, x, core))

    def pass_plus(cls, zs):
        return w_copy(cls, zs, y_down, 0, 4, device(y_up, z, half, x, core))

    def pass_minus(cls, zs):
        return w_copy(cls, zs, y_up, 1, 5, device(y_down, z, half, x, core))

    def send_y(cls, zs):
        y_plus(cls, zs, 0).start()
        y_minus(cls, zs, 1).start()
        y_plus(cls, zs, 1).start()
        y_minus(cls, zs, 0).start()

    def first_step(cls, spread):
        for part in range(2):

            @pl.when(z < 7)
            def _():
                z_right(cls, z, part).start()

            @pl.when(z > 0)
            def _():
                z_left(cls, z, part).start()

        if spread:
            send_y(cls, z)

    def step(cls, s, spread):
        for part in range(2):

            @pl.when(z >= s)
            def _():
                w_wait(cls, z - s, y, part)

                @pl.when(z < 7)
                def _():
                    z_right(cls, z - s, part).start()

            @pl.when(z + s <= 7)
            def _():
                w_wait(cls, z + s, y, part)

                @pl.when(z > 0)
                def _():
                    z_left(cls, z + s, part).start()

        if spread:

            @pl.when(z >= s)
            def _():
                send_y(cls, z - s)

            @pl.when(z + s <= 7)
            def _():
                send_y(cls, z + s)

    def pass_one(cls, zs):
        w_wait(cls, zs, y_down, 0)
        pass_plus(cls, zs).start()
        w_wait(cls, zs, y_up, 1)
        pass_minus(cls, zs).start()

    def passes(cls, s):
        @pl.when(z >= s)
        def _():
            pass_one(cls, z - s)

        @pl.when((z + s <= 7) & (s > 0))
        def _():
            pass_one(cls, z + s)

    def finish(cls, zs):
        w_wait(cls, zs, y_down, 1)
        w_wait(cls, zs, y_up, 0)
        for part in range(2):
            w_wait(cls, zs, y_far, part)

    def sent(cls):
        @pl.loop(0, 8)
        def _(zs):
            for part in range(2):

                @pl.when((z < 7) & (zs <= z))
                def _():
                    z_right(cls, zs, part).wait_send()

                @pl.when((z > 0) & (zs >= z))
                def _():
                    z_left(cls, zs, part).wait_send()

                y_plus(cls, zs, part).wait_send()
                y_minus(cls, zs, part).wait_send()
            pass_plus(cls, zs).wait_send()
            pass_minus(cls, zs).wait_send()

    first_step(0, True)
    for p in range(2):
        tok_spread(half, p, 1)
    z8_copy(0).start()
    step(0, 1, True)
    z8_copy(1).start()
    step(0, 2, True)
    z8_copy(2).start()
    passes(0, 0)
    step(0, 3, True)
    z8_copy(3).start()
    passes(0, 1)
    for p in range(2):
        tok_pass(half, p, 5)
    step(0, 4, True)
    z8_copy(4).start()
    first_step(1, False)
    passes(0, 2)
    step(0, 5, True)
    step(1, 1, False)
    passes(0, 3)
    step(0, 6, True)
    step(1, 2, False)
    for k in range(5):
        z8_wait(k)
    for p in range(2):
        tok_spread(1 - half, p, 8)
    passes(0, 4)
    step(0, 7, True)
    step(1, 3, False)
    passes(0, 5)
    step(1, 4, False)
    passes(0, 6)
    step(1, 5, False)
    passes(0, 7)
    step(1, 6, False)
    tok_pass(1 - half, 0, 12)
    tok_pass(1 - half, 1, 12)
    step(1, 7, False)
    @pl.loop(0, 8)
    def _(s):
        @pl.when(z >= s)
        def _():
            send_y(1, z - s)

        @pl.when((z + s <= 7) & (s > 0))
        def _():
            send_y(1, z + s)


    @pl.loop(0, 8)
    def _(zs):
        finish(0, zs)
        rows = pl.ds(pl.multiple_of(zs * 400, 16), 400)
        for i in range(3):
            for p in range(2):
                wfull[i, rows, p * 128 : p * 128 + 128] = jnp.concatenate(
                    [abuf[zs * 4 + j, p, i * 100 : i * 100 + 100, :] for j in range(4)],
                    axis=0,
                )

    for h in range(2):
        for xx in range(4):
            for p in range(2):
                tok_wait(h, xx, 1 - core, p)

    keep = (
        tensor * 2 + lax.broadcasted_iota(jnp.int32, (1, 256), 1) // HD < HEADS
    ).astype(F32)

    def project(i):
        return jnp.dot(xg[...], wfull[i], preferred_element_type=F32) * keep

    sums = []
    for i in range(2):
        qkf[i] = project(i)
        sums.append(jnp.sum(qkf[i] * qkf[i], axis=1, keepdims=True))
    lane = lax.broadcasted_iota(jnp.int32, (512, 128), 1)
    stage[...] = jnp.where(
        lane == 0, sums[0], jnp.where(lane == 1, sums[1], 0.0)
    ).T
    spot = x * 2 + core
    for i in range(2):
        for j in range(4):
            srecv[spot, pl.ds(i * 4 + j, 1), :] = stage[i : i + 1, j * 128 : j * 128 + 128]

    def sum_copy(dx, other):
        return remote(
            srecv.at[spot], srecv.at[spot], s_send.at[dx * 2 + other],
            s_recv.at[spot], near(dx, other),
        )

    for dx in range(4):
        for other in range(2):
            if dx or other:
                sum_copy(dx, other).start()

    heads[2] = project(2).astype(BF16)

    @pl.loop(0, 4)
    def _(s):
        passes(1, s)

    for dx in range(4):
        for other in range(2):
            if dx or other:
                other_spot = ((x + dx) % 4) * 2 + (core + other) % 2
                arrived(srecv.at[other_spot], s_recv.at[other_spot])
    total = srecv[0]
    for i in range(1, 8):
        total += srecv[i]
    sown[...] = total
    across_sum = remote(sown, szrecv, s_send.at[0], s_recv.at[8], across)
    for dx in range(4):
        for other in range(2):
            if dx or other:
                sum_copy(dx, other).wait_send()
    across_sum.start()

    @pl.loop(4, 8)
    def _(s):
        passes(1, s)

    across_sum.wait()
    total = sown[...] + szrecv[...]
    for i in range(2):
        for j in range(4):
            stage[i : i + 1, j * 128 : j * 128 + 128] = total[i * 4 + j : i * 4 + j + 1, :]
    columns = stage[...].T
    heads[0] = (
        qkf[0] * lax.rsqrt(columns[:, 0:1] / WIDTH + EPS) * qg_ref[...].reshape(1, 256)
    ).astype(BF16)
    heads[1] = (
        qkf[1] * lax.rsqrt(columns[:, 1:2] / WIDTH + EPS) * kg_ref[...].reshape(1, 256)
    ).astype(BF16)

    for h in range(2):
        cols = slice(h * HD, h * HD + HD)

        @pl.loop(0, 2)
        def _(r):
            rows = pl.ds(pl.multiple_of(r * 256, 256), 256)
            scores = lax.dot_general(
                heads[0, rows, cols], heads[1, :, cols], (((1,), (1,)), ((), ())),
                preferred_element_type=F32,
            ) * HD ** (-0.5)
            e = jnp.exp(scores - jnp.max(scores, axis=1, keepdims=True))
            probs = (e / jnp.sum(e, axis=1, keepdims=True)).astype(BF16)
            att[rows, cols] = jnp.dot(
                probs, heads[2, :, cols], preferred_element_type=F32
            ).astype(BF16)

    for k in range(5):
        z8_copy(k).wait_send()
    for slot in range(1, 15):
        for p in range(2):
            tok_copy(half, x, core, p, sibling, slot).wait_send()
    sent(0)

    @pl.loop(0, 8)
    def _(zs):
        finish(1, zs)
        rows = pl.ds(pl.multiple_of(zs * 400, 16), 400)
        for p in range(2):
            ofull[rows, p * 128 : p * 128 + 128] = jnp.concatenate(
                [bbuf[zs * 4 + j, p, 0:100, :] for j in range(4)], axis=0
            )

    x_up, x_down, x_far = (x + 1) % 4, (x + 3) % 4, (x + 2) % 4

    def to_sibling(c):
        return remote(
            terms[c].at[1 - core], rs1[c], r_send.at[c, 0], r_recv.at[c, 0], sibling
        )

    def far_copy(c, h):
        return remote(
            mid[c].at[x_far, h], far[c].at[h], r_send.at[c, 1 + h], r_recv.at[c, 1 + h],
            near(3 if h else 1, 0),
        )

    def plain_copy(c, h):
        return remote(
            mid[c].at[x_down if h == 0 else x_up, h], rs2[c].at[1 - h, h],
            r_send.at[c, 3 + h], r_recv.at[c, 3 + h], near(1 if h else 3, 0),
        )

    def added_copy(c, h):
        return remote(
            added[c].at[h], rs2[c].at[h, h], r_send.at[c, 5 + h], r_recv.at[c, 5 + h],
            near(3 if h else 1, 0),
        )

    def to_across(c):
        return remote(wsend[c], rs3[c], r_send.at[c, 7], r_recv.at[c, 7], across)

    def stage_one(c):
        part = lax.dot_general(
            att[...], ofull[STARTS[c] : STARTS[c] + COLS[c], :], (((1,), (1,)), ((), ())),
            preferred_element_type=F32,
        )
        terms[c][...] = part.astype(BF16).reshape(2, 256, COLS[c])
        to_sibling(c).start()

    def stage_two(c):
        to_sibling(c).wait_recv()
        both = (terms[c][core].astype(F32) + rs1[c][...].astype(F32)).astype(BF16)
        both = both.reshape(2, 4, 32, COLS[c])
        for xx in range(4):
            for h in range(2):
                mid[c][xx, h] = both[h, xx]
        for h in range(2):
            far_copy(c, h).start()
        for h in range(2):
            plain_copy(c, h).start()

    def stage_relay(c):
        for h in range(2):
            far_copy(c, h).wait_recv()
            mine_too = mid[c][x_down if h else x_up, h].astype(F32)
            added[c][h] = (mine_too + far[c][h].astype(F32)).astype(BF16)
            added_copy(c, h).start()

    def stage_three(c):
        for h in range(2):
            plain_copy(c, h).wait_recv()
            added_copy(c, h).wait_recv()

        def summed(h):
            s = mid[c][x, h].astype(F32)
            for side in range(2):
                s += rs2[c][side, h].astype(F32)
            return s

        wsend[c][...] = summed(1 - half).astype(BF16)
        to_across(c).start()
        wown[c][...] = summed(half)

    scale = ls_ref[...].reshape(1, D)

    def stage_four(c):
        to_across(c).wait_recv()
        cols = slice(STARTS[c], STARTS[c] + COLS[c])
        projected = wown[c][...] + rs3[c][...].astype(F32)
        out_ref[:, cols] = (
            tok_ref[:, cols].astype(F32) + scale[:, cols] * projected
        ).astype(BF16)

    for t in range(CHUNKS + 3):
        if t < CHUNKS:
            stage_one(t)
        if 0 <= t - 1 < CHUNKS:
            stage_two(t - 1)
        if 0 <= t - 2 < CHUNKS:
            stage_relay(t - 2)
        if 0 <= t - 3 < CHUNKS:
            stage_three(t - 3)
    for c in range(CHUNKS):
        stage_four(c)

    sent(1)
    for c in range(CHUNKS):
        to_sibling(c).wait_send()
        for h in range(2):
            far_copy(c, h).wait_send()
            plain_copy(c, h).wait_send()
            added_copy(c, h).wait_send()
        to_across(c).wait_send()


def chunked(dtype, *dims):
    return [pltpu.VMEM((*dims, cols), dtype) for cols in COLS]


def shards(tokens, norm_gain, qkv_weight, q_gain, k_gain, out_weight, layer_scale):
    vmem = pl.BlockSpec(memory_space=pltpu.VMEM)
    dma = pltpu.SemaphoreType.DMA
    return pl.pallas_call(
        kernel,
        out_shape=jax.ShapeDtypeStruct((32, D), BF16),
        in_specs=[vmem] * 7,
        out_specs=vmem,
        scratch_shapes=[
            pltpu.VMEM((512, D), BF16),
            pltpu.VMEM((32, 2, QKV_ROWS, 128), BF16),
            pltpu.VMEM((32, 2, OUT_ROWS, 128), BF16),
            pltpu.VMEM((3, D, 256), BF16),
            pltpu.VMEM((D, 256), BF16),
            pltpu.VMEM((2, 512, 256), F32),
            pltpu.VMEM((3, 512, 256), BF16),
            pltpu.VMEM((512, 256), BF16),
            pltpu.VMEM((128, 512), F32),
            pltpu.VMEM((8, 8, 128), F32),
            pltpu.VMEM((8, 128), F32),
            pltpu.VMEM((8, 128), F32),
            *chunked(BF16, 2, 256),
            *chunked(BF16, 256),
            *chunked(BF16, 4, 2, 32),
            *chunked(BF16, 2, 32),
            *chunked(BF16, 2, 32),
            *chunked(BF16, 2, 2, 32),
            *chunked(F32, 32),
            *chunked(BF16, 32),
            *chunked(BF16, 32),
            dma((16, 2)),
            dma((15, 2)),
            dma((5,)),
            dma((5,)),
            dma((2, 32, 2)),
            dma((2, 6, 8, 2)),
            dma((9,)),
            dma((8,)),
            dma((CHUNKS, 8)),
            dma((CHUNKS, 8)),
        ],
        compiler_params=pltpu.CompilerParams(
            collective_id=0, has_side_effects=True, vmem_limit_bytes=60 * 1024 * 1024
        ),
        cost_estimate=pl.CostEstimate(
            flops=4_000_000_000, bytes_accessed=1_000_000, transcendentals=600_000
        ),
    )(
        tokens, norm_gain, qkv_weight, out_weight.T, q_gain, k_gain, layer_scale
    )


def solution(mesh):
    placed = (
        P(("dp", "tensor"), None),
        P(),
        P(None, "dp", "tensor"),
        P("tensor"),
        P("tensor"),
        P("tensor", "dp"),
        P(),
    )
    return jax.shard_map(
        shards, mesh=mesh, in_specs=placed, out_specs=P(("dp", "tensor"), None), check_vma=False
    )
```

```python
import jax
import jax.numpy as jnp
from jax import lax
from jax.experimental import pallas as pl
from jax.experimental.pallas import tpu as pltpu
from jax.sharding import PartitionSpec as P

D = 3200
HEADS = 25
HD = 128
EPS = 1e-06
WIDTH = HEADS * HD
QKV_ROWS = 304
OUT_ROWS = 112
COLS = (640, 640, 640, 640, 640)
CHUNKS = len(COLS)
STARTS = tuple(sum(COLS[:c]) for c in range(CHUNKS))
MESH = pl.DeviceIdType.MESH
F32 = jnp.float32
BF16 = jnp.bfloat16


def device(y, z, half, x, core):
    return (z * 4 + y, half * 8 + x * 2 + core)


def kernel(*refs):
    tok_ref, gain_ref, qkv_ref, o_ref, qg_ref, kg_ref, ls_ref, out_ref = refs[:8]
    xg, abuf, bbuf, wfull, ofull, qkf, heads, att, stage, srecv, szrecv, sown = refs[8:20]
    chunk_refs = refs[20:-10]
    terms, rs1, mid, far, added, rs2, wown, wsend, rs3 = [
        chunk_refs[i * CHUNKS : (i + 1) * CHUNKS] for i in range(9)
    ]
    tok_recv, tok_send, z8_recv, z8_send, w_recv, w_send = refs[-10:-4]
    s_recv, s_send, r_recv, r_send = refs[-4:]
    dp = lax.axis_index("dp")
    tensor = lax.axis_index("tensor")
    y, z = dp % 4, dp // 4
    half, x, core = tensor // 8, (tensor // 2) % 4, tensor % 2
    y_up, y_down, y_far = (y + 1) % 4, (y + 3) % 4, (y + 2) % 4
    sibling = device(y, z, half, x, 1 - core)
    across = device(y, z, 1 - half, x, core)

    def near(dx, other):
        c = (core + other) % 2
        return device(y, z, half, (x + dx) % 4, c)

    barrier = pltpu.get_barrier_semaphore()

    def greet(target):
        pl.semaphore_signal(barrier, 1, device_id=target, device_id_type=MESH)

    greet(across)
    greet(device(y_up, z, half, x, core))
    greet(device(y_down, z, half, x, core))
    for dx in range(4):
        for other in range(2):
            if dx or other:
                greet(near(dx, other))

    @pl.when(z > 0)
    def _():
        greet(device(y, z - 1, half, x, core))

    @pl.when(z < 7)
    def _():
        greet(device(y, z + 1, half, x, core))

    def remote(src, dst, send, recv, target):
        return pltpu.make_async_remote_copy(
            src_ref=src, dst_ref=dst, send_sem=send, recv_sem=recv,
            device_id=target, device_id_type=MESH,
        )

    def arrived(ref, sem):
        pltpu.make_async_copy(ref, ref, sem).wait()

    def row_block(h, xx, c, p):
        return pl.ds(pl.multiple_of(c * 256 + h * 128 + xx * 32 + p * 16, 16), 16)

    tok = tok_ref[...].astype(F32)
    sq = jnp.sum(tok * tok, axis=1, keepdims=True)
    normed = (
        tok * lax.rsqrt(sq / D + EPS) * gain_ref[...].astype(F32).reshape(1, D)
    ).astype(BF16)
    for p in range(2):
        xg[row_block(half, x, core, p), :] = normed[p * 16 : p * 16 + 16, :]
    mine = z * 4 + y
    for p in range(2):
        cols = slice(p * 128, p * 128 + 128)
        abuf[mine, p] = jnp.concatenate(
            [qkv_ref[i, :, cols] for i in range(3)]
            + [jnp.zeros((QKV_ROWS - 300, 128), BF16)],
            axis=0,
        )
    for p in range(2):
        bbuf[mine, p] = jnp.concatenate(
            [
                o_ref[:, p * 128 : p * 128 + 128],
                jnp.zeros((OUT_ROWS - 100, 128), BF16),
            ],
            axis=0,
        )

    pl.semaphore_wait(
        barrier, 10 + (z > 0).astype(jnp.int32) + (z < 7).astype(jnp.int32)
    )

    def tok_copy(h, xx, c, p, target, slot):
        ref = xg.at[row_block(h, xx, c, p), :]
        return remote(
            ref, ref, tok_send.at[slot, p], tok_recv.at[h * 8 + xx * 2 + c, p], target
        )

    def tok_wait(h, xx, c, p):
        arrived(xg.at[row_block(h, xx, c, p), :], tok_recv.at[h * 8 + xx * 2 + c, p])

    def tok_spread(h, p, base):
        for dx in (2, 1, 3):
            tok_copy(h, x, core, p, near(dx, 0), base + dx - 1).start()
        tok_copy(h, x, core, p, sibling, base + 3).start()

    def tok_pass(h, p, base):
        for dx in (1, 3, 2):
            xx = (x + dx) % 4
            tok_wait(h, xx, core, p)
            tok_copy(h, xx, core, p, sibling, base + dx - 1).start()


    def z8_copy(k):
        ref = xg.at[pl.ds(pl.multiple_of(core * 256 + half * 128 + x * 32, 32), 32), pl.ds(k * 640, 640)]
        return remote(ref, ref, z8_send.at[k], z8_recv.at[k], across)

    def z8_wait(k):
        ref = xg.at[pl.ds(pl.multiple_of(core * 256 + (1 - half) * 128 + x * 32, 32), 32), pl.ds(k * 640, 640)]
        arrived(ref, z8_recv.at[k])

    bufs = (abuf, bbuf)

    def w_copy(cls, zs, yy, part, kind, target):
        b = zs * 4 + yy
        ref = bufs[cls].at[b, part]
        return remote(
            ref, ref, w_send.at[cls, kind, zs, part], w_recv.at[cls, b, part], target
        )

    def w_wait(cls, zs, yy, part):
        b = zs * 4 + yy
        arrived(bufs[cls].at[b, part], w_recv.at[cls, b, part])

    def z_right(cls, zs, part):
        return w_copy(cls, zs, y, part, 0, device(y, z + 1, half, x, core))

    def z_left(cls, zs, part):
        return w_copy(cls, zs, y, part, 1, device(y, z - 1, half, x, core))

    def y_plus(cls, zs, part):
        return w_copy(cls, zs, y, part, 2, device(y_up, z, half, x, core))

    def y_minus(cls, zs, part):
        return w_copy(cls, zs, y, part, 3, device(y_down, z, half, x, core))

    def pass_plus(cls, zs):
        return w_copy(cls, zs, y_down, 0, 4, device(y_up, z, half, x, core))

    def pass_minus(cls, zs):
        return w_copy(cls, zs, y_up, 1, 5, device(y_down, z, half, x, core))

    def send_y(cls, zs):
        y_plus(cls, zs, 0).start()
        y_minus(cls, zs, 1).start()
        y_plus(cls, zs, 1).start()
        y_minus(cls, zs, 0).start()

    def first_step(cls, spread):
        for part in range(2):

            @pl.when(z < 7)
            def _():
                z_right(cls, z, part).start()

            @pl.when(z > 0)
            def _():
                z_left(cls, z, part).start()

        if spread:
            send_y(cls, z)

    def step(cls, s, spread):
        for part in range(2):

            @pl.when(z >= s)
            def _():
                w_wait(cls, z - s, y, part)

                @pl.when(z < 7)
                def _():
                    z_right(cls, z - s, part).start()

            @pl.when(z + s <= 7)
            def _():
                w_wait(cls, z + s, y, part)

                @pl.when(z > 0)
                def _():
                    z_left(cls, z + s, part).start()

        if spread:

            @pl.when(z >= s)
            def _():
                send_y(cls, z - s)

            @pl.when(z + s <= 7)
            def _():
                send_y(cls, z + s)

    def pass_one(cls, zs):
        w_wait(cls, zs, y_down, 0)
        pass_plus(cls, zs).start()
        w_wait(cls, zs, y_up, 1)
        pass_minus(cls, zs).start()

    def passes(cls, s):
        @pl.when(z >= s)
        def _():
            pass_one(cls, z - s)

        @pl.when((z + s <= 7) & (s > 0))
        def _():
            pass_one(cls, z + s)

    def finish(cls, zs):
        w_wait(cls, zs, y_down, 1)
        w_wait(cls, zs, y_up, 0)
        for part in range(2):
            w_wait(cls, zs, y_far, part)

    def sent(cls):
        @pl.loop(0, 8)
        def _(zs):
            for part in range(2):

                @pl.when((z < 7) & (zs <= z))
                def _():
                    z_right(cls, zs, part).wait_send()

                @pl.when((z > 0) & (zs >= z))
                def _():
                    z_left(cls, zs, part).wait_send()

                y_plus(cls, zs, part).wait_send()
                y_minus(cls, zs, part).wait_send()
            pass_plus(cls, zs).wait_send()
            pass_minus(cls, zs).wait_send()

    first_step(0, True)
    for p in range(2):
        tok_spread(half, p, 1)
    z8_copy(0).start()
    step(0, 1, True)
    z8_copy(1).start()
    step(0, 2, True)
    z8_copy(2).start()
    passes(0, 0)
    step(0, 3, True)
    z8_copy(3).start()
    passes(0, 1)
    for p in range(2):
        tok_pass(half, p, 5)
    step(0, 4, True)
    z8_copy(4).start()
    first_step(1, False)
    passes(0, 2)
    step(0, 5, True)
    step(1, 1, False)
    passes(0, 3)
    step(0, 6, True)
    step(1, 2, False)
    for k in range(5):
        z8_wait(k)
    for p in range(2):
        tok_spread(1 - half, p, 8)
    passes(0, 4)
    step(0, 7, True)
    step(1, 3, False)
    passes(0, 5)
    step(1, 4, False)
    passes(0, 6)
    step(1, 5, False)
    passes(0, 7)
    step(1, 6, False)
    tok_pass(1 - half, 0, 12)
    tok_pass(1 - half, 1, 12)
    step(1, 7, False)
    @pl.loop(0, 8)
    def _(s):
        @pl.when(z >= s)
        def _():
            send_y(1, z - s)

        @pl.when((z + s <= 7) & (s > 0))
        def _():
            send_y(1, z + s)


    @pl.loop(0, 8)
    def _(zs):
        finish(0, zs)
        rows = pl.ds(pl.multiple_of(zs * 400, 16), 400)
        for i in range(3):
            for p in range(2):
                wfull[i, rows, p * 128 : p * 128 + 128] = jnp.concatenate(
                    [abuf[zs * 4 + j, p, i * 100 : i * 100 + 100, :] for j in range(4)],
                    axis=0,
                )

    for h in range(2):
        for xx in range(4):
            for p in range(2):
                tok_wait(h, xx, 1 - core, p)

    keep = (
        tensor * 2 + lax.broadcasted_iota(jnp.int32, (1, 256), 1) // HD < HEADS
    ).astype(F32)

    def project(i):
        return jnp.dot(xg[...], wfull[i], preferred_element_type=F32) * keep

    sums = []
    for i in range(2):
        qkf[i] = project(i)
        sums.append(jnp.sum(qkf[i] * qkf[i], axis=1, keepdims=True))
    lane = lax.broadcasted_iota(jnp.int32, (512, 128), 1)
    stage[...] = jnp.where(
        lane == 0, sums[0], jnp.where(lane == 1, sums[1], 0.0)
    ).T
    spot = x * 2 + core
    for i in range(2):
        for j in range(4):
            srecv[spot, pl.ds(i * 4 + j, 1), :] = stage[i : i + 1, j * 128 : j * 128 + 128]

    def sum_copy(dx, other):
        return remote(
            srecv.at[spot], srecv.at[spot], s_send.at[dx * 2 + other],
            s_recv.at[spot], near(dx, other),
        )

    for dx in range(4):
        for other in range(2):
            if dx or other:
                sum_copy(dx, other).start()

    heads[2] = project(2).astype(BF16)

    @pl.loop(0, 4)
    def _(s):
        passes(1, s)

    for dx in range(4):
        for other in range(2):
            if dx or other:
                other_spot = ((x + dx) % 4) * 2 + (core + other) % 2
                arrived(srecv.at[other_spot], s_recv.at[other_spot])
    total = srecv[0]
    for i in range(1, 8):
        total += srecv[i]
    sown[...] = total
    across_sum = remote(sown, szrecv, s_send.at[0], s_recv.at[8], across)
    for dx in range(4):
        for other in range(2):
            if dx or other:
                sum_copy(dx, other).wait_send()
    across_sum.start()

    @pl.loop(4, 8)
    def _(s):
        passes(1, s)

    across_sum.wait()
    total = sown[...] + szrecv[...]
    for i in range(2):
        for j in range(4):
            stage[i : i + 1, j * 128 : j * 128 + 128] = total[i * 4 + j : i * 4 + j + 1, :]
    columns = stage[...].T
    heads[0] = (
        qkf[0] * lax.rsqrt(columns[:, 0:1] / WIDTH + EPS) * qg_ref[...].reshape(1, 256)
    ).astype(BF16)
    heads[1] = (
        qkf[1] * lax.rsqrt(columns[:, 1:2] / WIDTH + EPS) * kg_ref[...].reshape(1, 256)
    ).astype(BF16)

    for h in range(2):
        cols = slice(h * HD, h * HD + HD)

        @pl.loop(0, 2)
        def _(r):
            rows = pl.ds(pl.multiple_of(r * 256, 256), 256)
            scores = lax.dot_general(
                heads[0, rows, cols], heads[1, :, cols], (((1,), (1,)), ((), ())),
                preferred_element_type=F32,
            ) * HD ** (-0.5)
            e = jnp.exp(scores - jnp.max(scores, axis=1, keepdims=True))
            probs = (e / jnp.sum(e, axis=1, keepdims=True)).astype(BF16)
            att[rows, cols] = jnp.dot(
                probs, heads[2, :, cols], preferred_element_type=F32
            ).astype(BF16)

    for k in range(5):
        z8_copy(k).wait_send()
    for slot in range(1, 15):
        for p in range(2):
            tok_copy(half, x, core, p, sibling, slot).wait_send()
    sent(0)

    @pl.loop(0, 8)
    def _(zs):
        finish(1, zs)
        rows = pl.ds(pl.multiple_of(zs * 400, 16), 400)
        for p in range(2):
            ofull[rows, p * 128 : p * 128 + 128] = jnp.concatenate(
                [bbuf[zs * 4 + j, p, 0:100, :] for j in range(4)], axis=0
            )

    x_up, x_down, x_far = (x + 1) % 4, (x + 3) % 4, (x + 2) % 4

    def to_sibling(c):
        return remote(
            terms[c].at[1 - core], rs1[c], r_send.at[c, 0], r_recv.at[c, 0], sibling
        )

    def far_copy(c, h):
        return remote(
            mid[c].at[x_far, h], far[c].at[h], r_send.at[c, 1 + h], r_recv.at[c, 1 + h],
            near(3 if h else 1, 0),
        )

    def plain_copy(c, h):
        return remote(
            mid[c].at[x_down if h == 0 else x_up, h], rs2[c].at[1 - h, h],
            r_send.at[c, 3 + h], r_recv.at[c, 3 + h], near(1 if h else 3, 0),
        )

    def added_copy(c, h):
        return remote(
            added[c].at[h], rs2[c].at[h, h], r_send.at[c, 5 + h], r_recv.at[c, 5 + h],
            near(3 if h else 1, 0),
        )

    def to_across(c):
        return remote(wsend[c], rs3[c], r_send.at[c, 7], r_recv.at[c, 7], across)

    def stage_one(c):
        part = lax.dot_general(
            att[...], ofull[STARTS[c] : STARTS[c] + COLS[c], :], (((1,), (1,)), ((), ())),
            preferred_element_type=F32,
        )
        terms[c][...] = part.astype(BF16).reshape(2, 256, COLS[c])
        to_sibling(c).start()

    def stage_two(c):
        to_sibling(c).wait_recv()
        both = (terms[c][core].astype(F32) + rs1[c][...].astype(F32)).astype(BF16)
        both = both.reshape(2, 4, 32, COLS[c])
        for xx in range(4):
            for h in range(2):
                mid[c][xx, h] = both[h, xx]
        for h in range(2):
            far_copy(c, h).start()
        for h in range(2):
            plain_copy(c, h).start()

    def stage_relay(c):
        for h in range(2):
            far_copy(c, h).wait_recv()
            mine_too = mid[c][x_down if h else x_up, h].astype(F32)
            added[c][h] = (mine_too + far[c][h].astype(F32)).astype(BF16)
            added_copy(c, h).start()

    def stage_three(c):
        for h in range(2):
            plain_copy(c, h).wait_recv()
            added_copy(c, h).wait_recv()

        def summed(h):
            s = mid[c][x, h].astype(F32)
            for side in range(2):
                s += rs2[c][side, h].astype(F32)
            return s

        wsend[c][...] = summed(1 - half).astype(BF16)
        to_across(c).start()
        wown[c][...] = summed(half)

    scale = ls_ref[...].reshape(1, D)

    def stage_four(c):
        to_across(c).wait_recv()
        cols = slice(STARTS[c], STARTS[c] + COLS[c])
        projected = wown[c][...] + rs3[c][...].astype(F32)
        out_ref[:, cols] = (
            tok_ref[:, cols].astype(F32) + scale[:, cols] * projected
        ).astype(BF16)

    for t in range(CHUNKS + 3):
        if t < CHUNKS:
            stage_one(t)
        if 0 <= t - 1 < CHUNKS:
            stage_two(t - 1)
        if 0 <= t - 2 < CHUNKS:
            stage_relay(t - 2)
        if 0 <= t - 3 < CHUNKS:
            stage_three(t - 3)
    for c in range(CHUNKS):
        stage_four(c)

    sent(1)
    for c in range(CHUNKS):
        to_sibling(c).wait_send()
        for h in range(2):
            far_copy(c, h).wait_send()
            plain_copy(c, h).wait_send()
            added_copy(c, h).wait_send()
        to_across(c).wait_send()


def chunked(dtype, *dims):
    return [pltpu.VMEM((*dims, cols), dtype) for cols in COLS]


def shards(tokens, norm_gain, qkv_weight, q_gain, k_gain, out_weight, layer_scale):
    vmem = pl.BlockSpec(memory_space=pltpu.VMEM)
    dma = pltpu.SemaphoreType.DMA
    return pl.pallas_call(
        kernel,
        out_shape=jax.ShapeDtypeStruct((32, D), BF16),
        in_specs=[vmem] * 7,
        out_specs=vmem,
        scratch_shapes=[
            pltpu.VMEM((512, D), BF16),
            pltpu.VMEM((32, 2, QKV_ROWS, 128), BF16),
            pltpu.VMEM((32, 2, OUT_ROWS, 128), BF16),
            pltpu.VMEM((3, D, 256), BF16),
            pltpu.VMEM((D, 256), BF16),
            pltpu.VMEM((2, 512, 256), F32),
            pltpu.VMEM((3, 512, 256), BF16),
            pltpu.VMEM((512, 256), BF16),
            pltpu.VMEM((128, 512), F32),
            pltpu.VMEM((8, 8, 128), F32),
            pltpu.VMEM((8, 128), F32),
            pltpu.VMEM((8, 128), F32),
            *chunked(BF16, 2, 256),
            *chunked(BF16, 256),
            *chunked(BF16, 4, 2, 32),
            *chunked(BF16, 2, 32),
            *chunked(BF16, 2, 32),
            *chunked(BF16, 2, 2, 32),
            *chunked(F32, 32),
            *chunked(BF16, 32),
            *chunked(BF16, 32),
            dma((16, 2)),
            dma((15, 2)),
            dma((5,)),
            dma((5,)),
            dma((2, 32, 2)),
            dma((2, 6, 8, 2)),
            dma((9,)),
            dma((8,)),
            dma((CHUNKS, 8)),
            dma((CHUNKS, 8)),
        ],
        compiler_params=pltpu.CompilerParams(
            collective_id=0, has_side_effects=True, vmem_limit_bytes=60 * 1024 * 1024
        ),
        cost_estimate=pl.CostEstimate(
            flops=4_000_000_000, bytes_accessed=1_000_000, transcendentals=600_000
        ),
    )(
        tokens, norm_gain, qkv_weight, out_weight.T, q_gain, k_gain, layer_scale
    )


def solution(mesh):
    placed = (
        P(("dp", "tensor"), None),
        P(),
        P(None, "dp", "tensor"),
        P("tensor"),
        P("tensor"),
        P("tensor", "dp"),
        P(),
    )
    return jax.shard_map(
        shards, mesh=mesh, in_specs=placed, out_specs=P(("dp", "tensor"), None), check_vma=False
    )
```

```python
import jax
import jax.numpy as jnp
from jax import lax
from jax.experimental import pallas as pl
from jax.experimental.pallas import tpu as pltpu
from jax.sharding import PartitionSpec as P

D = 3200
HEADS = 25
HD = 128
EPS = 1e-06
WIDTH = HEADS * HD
QKV_ROWS = 304
OUT_ROWS = 112
COLS = (640, 640, 640, 640, 640)
CHUNKS = len(COLS)
STARTS = tuple(sum(COLS[:c]) for c in range(CHUNKS))
MESH = pl.DeviceIdType.MESH
F32 = jnp.float32
BF16 = jnp.bfloat16


def device(y, z, half, x, core):
    return (z * 4 + y, half * 8 + x * 2 + core)


def kernel(*refs):
    tok_ref, gain_ref, qkv_ref, o_ref, qg_ref, kg_ref, ls_ref, out_ref = refs[:8]
    xg, abuf, bbuf, wfull, ofull, qkf, heads, att, stage, srecv, szrecv, sown = refs[8:20]
    chunk_refs = refs[20:-10]
    terms, rs1, mid, far, added, rs2, wown, wsend, rs3 = [
        chunk_refs[i * CHUNKS : (i + 1) * CHUNKS] for i in range(9)
    ]
    tok_recv, tok_send, z8_recv, z8_send, w_recv, w_send = refs[-10:-4]
    s_recv, s_send, r_recv, r_send = refs[-4:]
    dp = lax.axis_index("dp")
    tensor = lax.axis_index("tensor")
    y, z = dp % 4, dp // 4
    half, x, core = tensor // 8, (tensor // 2) % 4, tensor % 2
    y_up, y_down, y_far = (y + 1) % 4, (y + 3) % 4, (y + 2) % 4
    sibling = device(y, z, half, x, 1 - core)
    across = device(y, z, 1 - half, x, core)

    def near(dx, other):
        c = (core + other) % 2
        return device(y, z, half, (x + dx) % 4, c)

    barrier = pltpu.get_barrier_semaphore()

    def greet(target):
        pl.semaphore_signal(barrier, 1, device_id=target, device_id_type=MESH)

    greet(across)
    greet(device(y_up, z, half, x, core))
    greet(device(y_down, z, half, x, core))
    for dx in range(4):
        for other in range(2):
            if dx or other:
                greet(near(dx, other))

    @pl.when(z > 0)
    def _():
        greet(device(y, z - 1, half, x, core))

    @pl.when(z < 7)
    def _():
        greet(device(y, z + 1, half, x, core))

    def remote(src, dst, send, recv, target):
        return pltpu.make_async_remote_copy(
            src_ref=src, dst_ref=dst, send_sem=send, recv_sem=recv,
            device_id=target, device_id_type=MESH,
        )

    def arrived(ref, sem):
        pltpu.make_async_copy(ref, ref, sem).wait()

    def row_block(h, xx, c, p):
        return pl.ds(pl.multiple_of(c * 256 + h * 128 + xx * 32 + p * 16, 16), 16)

    tok = tok_ref[...].astype(F32)
    sq = jnp.sum(tok * tok, axis=1, keepdims=True)
    normed = (
        tok * lax.rsqrt(sq / D + EPS) * gain_ref[...].astype(F32).reshape(1, D)
    ).astype(BF16)
    for p in range(2):
        xg[row_block(half, x, core, p), :] = normed[p * 16 : p * 16 + 16, :]
    mine = z * 4 + y
    for p in range(2):
        cols = slice(p * 128, p * 128 + 128)
        abuf[mine, p] = jnp.concatenate(
            [qkv_ref[i, :, cols] for i in range(3)]
            + [jnp.zeros((QKV_ROWS - 300, 128), BF16)],
            axis=0,
        )
    for p in range(2):
        bbuf[mine, p] = jnp.concatenate(
            [
                o_ref[:, p * 128 : p * 128 + 128],
                jnp.zeros((OUT_ROWS - 100, 128), BF16),
            ],
            axis=0,
        )

    pl.semaphore_wait(
        barrier, 10 + (z > 0).astype(jnp.int32) + (z < 7).astype(jnp.int32)
    )

    def tok_copy(h, xx, c, p, target, slot):
        ref = xg.at[row_block(h, xx, c, p), :]
        return remote(
            ref, ref, tok_send.at[slot, p], tok_recv.at[h * 8 + xx * 2 + c, p], target
        )

    def tok_wait(h, xx, c, p):
        arrived(xg.at[row_block(h, xx, c, p), :], tok_recv.at[h * 8 + xx * 2 + c, p])

    def tok_spread(h, p, base):
        for dx in (2, 1, 3):
            tok_copy(h, x, core, p, near(dx, 0), base + dx - 1).start()
        tok_copy(h, x, core, p, sibling, base + 3).start()

    def tok_pass(h, p, base):
        for dx in (1, 3, 2):
            xx = (x + dx) % 4
            tok_wait(h, xx, core, p)
            tok_copy(h, xx, core, p, sibling, base + dx - 1).start()


    def z8_copy(k):
        ref = xg.at[pl.ds(pl.multiple_of(core * 256 + half * 128 + x * 32, 32), 32), pl.ds(k * 640, 640)]
        return remote(ref, ref, z8_send.at[k], z8_recv.at[k], across)

    def z8_wait(k):
        ref = xg.at[pl.ds(pl.multiple_of(core * 256 + (1 - half) * 128 + x * 32, 32), 32), pl.ds(k * 640, 640)]
        arrived(ref, z8_recv.at[k])

    bufs = (abuf, bbuf)

    def w_copy(cls, zs, yy, part, kind, target):
        b = zs * 4 + yy
        ref = bufs[cls].at[b, part]
        return remote(
            ref, ref, w_send.at[cls, kind, zs, part], w_recv.at[cls, b, part], target
        )

    def w_wait(cls, zs, yy, part):
        b = zs * 4 + yy
        arrived(bufs[cls].at[b, part], w_recv.at[cls, b, part])

    def z_right(cls, zs, part):
        return w_copy(cls, zs, y, part, 0, device(y, z + 1, half, x, core))

    def z_left(cls, zs, part):
        return w_copy(cls, zs, y, part, 1, device(y, z - 1, half, x, core))

    def y_plus(cls, zs, part):
        return w_copy(cls, zs, y, part, 2, device(y_up, z, half, x, core))

    def y_minus(cls, zs, part):
        return w_copy(cls, zs, y, part, 3, device(y_down, z, half, x, core))

    def pass_plus(cls, zs):
        return w_copy(cls, zs, y_down, 0, 4, device(y_up, z, half, x, core))

    def pass_minus(cls, zs):
        return w_copy(cls, zs, y_up, 1, 5, device(y_down, z, half, x, core))

    def send_y(cls, zs):
        y_plus(cls, zs, 0).start()
        y_minus(cls, zs, 1).start()
        y_plus(cls, zs, 1).start()
        y_minus(cls, zs, 0).start()

    def first_step(cls, spread):
        for part in range(2):

            @pl.when(z < 7)
            def _():
                z_right(cls, z, part).start()

            @pl.when(z > 0)
            def _():
                z_left(cls, z, part).start()

        if spread:
            send_y(cls, z)

    def step(cls, s, spread):
        for part in range(2):

            @pl.when(z >= s)
            def _():
                w_wait(cls, z - s, y, part)

                @pl.when(z < 7)
                def _():
                    z_right(cls, z - s, part).start()

            @pl.when(z + s <= 7)
            def _():
                w_wait(cls, z + s, y, part)

                @pl.when(z > 0)
                def _():
                    z_left(cls, z + s, part).start()

        if spread:

            @pl.when(z >= s)
            def _():
                send_y(cls, z - s)

            @pl.when(z + s <= 7)
            def _():
                send_y(cls, z + s)

    def pass_one(cls, zs):
        w_wait(cls, zs, y_down, 0)
        pass_plus(cls, zs).start()
        w_wait(cls, zs, y_up, 1)
        pass_minus(cls, zs).start()

    def passes(cls, s):
        @pl.when(z >= s)
        def _():
            pass_one(cls, z - s)

        @pl.when((z + s <= 7) & (s > 0))
        def _():
            pass_one(cls, z + s)

    def finish(cls, zs):
        w_wait(cls, zs, y_down, 1)
        w_wait(cls, zs, y_up, 0)
        for part in range(2):
            w_wait(cls, zs, y_far, part)

    def sent(cls):
        @pl.loop(0, 8)
        def _(zs):
            for part in range(2):

                @pl.when((z < 7) & (zs <= z))
                def _():
                    z_right(cls, zs, part).wait_send()

                @pl.when((z > 0) & (zs >= z))
                def _():
                    z_left(cls, zs, part).wait_send()

                y_plus(cls, zs, part).wait_send()
                y_minus(cls, zs, part).wait_send()
            pass_plus(cls, zs).wait_send()
            pass_minus(cls, zs).wait_send()

    first_step(0, True)
    for p in range(2):
        tok_spread(half, p, 1)
    z8_copy(0).start()
    step(0, 1, True)
    z8_copy(1).start()
    step(0, 2, True)
    z8_copy(2).start()
    passes(0, 0)
    step(0, 3, True)
    z8_copy(3).start()
    passes(0, 1)
    for p in range(2):
        tok_pass(half, p, 5)
    step(0, 4, True)
    z8_copy(4).start()
    first_step(1, False)
    passes(0, 2)
    step(0, 5, True)
    step(1, 1, False)
    passes(0, 3)
    step(0, 6, True)
    step(1, 2, False)
    for k in range(5):
        z8_wait(k)
    for p in range(2):
        tok_spread(1 - half, p, 8)
    passes(0, 4)
    step(0, 7, True)
    step(1, 3, False)
    passes(0, 5)
    step(1, 4, False)
    passes(0, 6)
    step(1, 5, False)
    passes(0, 7)
    step(1, 6, False)
    tok_pass(1 - half, 0, 12)
    tok_pass(1 - half, 1, 12)
    step(1, 7, False)
    @pl.loop(0, 8)
    def _(s):
        @pl.when(z >= s)
        def _():
            send_y(1, z - s)

        @pl.when((z + s <= 7) & (s > 0))
        def _():
            send_y(1, z + s)


    @pl.loop(0, 8)
    def _(zs):
        finish(0, zs)
        rows = pl.ds(pl.multiple_of(zs * 400, 16), 400)
        for i in range(3):
            for p in range(2):
                wfull[i, rows, p * 128 : p * 128 + 128] = jnp.concatenate(
                    [abuf[zs * 4 + j, p, i * 100 : i * 100 + 100, :] for j in range(4)],
                    axis=0,
                )

    for h in range(2):
        for xx in range(4):
            for p in range(2):
                tok_wait(h, xx, 1 - core, p)

    keep = (
        tensor * 2 + lax.broadcasted_iota(jnp.int32, (1, 256), 1) // HD < HEADS
    ).astype(F32)

    def project(i):
        return jnp.dot(xg[...], wfull[i], preferred_element_type=F32) * keep

    sums = []
    for i in range(2):
        qkf[i] = project(i)
        sums.append(jnp.sum(qkf[i] * qkf[i], axis=1, keepdims=True))
    lane = lax.broadcasted_iota(jnp.int32, (512, 128), 1)
    stage[...] = jnp.where(
        lane == 0, sums[0], jnp.where(lane == 1, sums[1], 0.0)
    ).T
    spot = x * 2 + core
    for i in range(2):
        for j in range(4):
            srecv[spot, pl.ds(i * 4 + j, 1), :] = stage[i : i + 1, j * 128 : j * 128 + 128]

    def sum_copy(dx, other):
        return remote(
            srecv.at[spot], srecv.at[spot], s_send.at[dx * 2 + other],
            s_recv.at[spot], near(dx, other),
        )

    for dx in range(4):
        for other in range(2):
            if dx or other:
                sum_copy(dx, other).start()

    heads[2] = project(2).astype(BF16)

    @pl.loop(0, 4)
    def _(s):
        passes(1, s)

    for dx in range(4):
        for other in range(2):
            if dx or other:
                other_spot = ((x + dx) % 4) * 2 + (core + other) % 2
                arrived(srecv.at[other_spot], s_recv.at[other_spot])
    total = srecv[0]
    for i in range(1, 8):
        total += srecv[i]
    sown[...] = total
    across_sum = remote(sown, szrecv, s_send.at[0], s_recv.at[8], across)
    for dx in range(4):
        for other in range(2):
            if dx or other:
                sum_copy(dx, other).wait_send()
    across_sum.start()

    @pl.loop(4, 8)
    def _(s):
        passes(1, s)

    across_sum.wait()
    total = sown[...] + szrecv[...]
    for i in range(2):
        for j in range(4):
            stage[i : i + 1, j * 128 : j * 128 + 128] = total[i * 4 + j : i * 4 + j + 1, :]
    columns = stage[...].T
    heads[0] = (
        qkf[0] * lax.rsqrt(columns[:, 0:1] / WIDTH + EPS) * qg_ref[...].reshape(1, 256)
    ).astype(BF16)
    heads[1] = (
        qkf[1] * lax.rsqrt(columns[:, 1:2] / WIDTH + EPS) * kg_ref[...].reshape(1, 256)
    ).astype(BF16)

    for h in range(2):
        cols = slice(h * HD, h * HD + HD)

        @pl.loop(0, 2)
        def _(r):
            rows = pl.ds(pl.multiple_of(r * 256, 256), 256)
            scores = lax.dot_general(
                heads[0, rows, cols], heads[1, :, cols], (((1,), (1,)), ((), ())),
                preferred_element_type=F32,
            ) * HD ** (-0.5)
            e = jnp.exp(scores - jnp.max(scores, axis=1, keepdims=True))
            probs = (e / jnp.sum(e, axis=1, keepdims=True)).astype(BF16)
            att[rows, cols] = jnp.dot(
                probs, heads[2, :, cols], preferred_element_type=F32
            ).astype(BF16)

    @pl.loop(0, 8)
    def _(zs):
        finish(1, zs)
        rows = pl.ds(pl.multiple_of(zs * 400, 16), 400)
        for p in range(2):
            ofull[rows, p * 128 : p * 128 + 128] = jnp.concatenate(
                [bbuf[zs * 4 + j, p, 0:100, :] for j in range(4)], axis=0
            )

    x_up, x_down, x_far = (x + 1) % 4, (x + 3) % 4, (x + 2) % 4

    def to_sibling(c):
        return remote(
            terms[c].at[1 - core], rs1[c], r_send.at[c, 0], r_recv.at[c, 0], sibling
        )

    def far_copy(c, h):
        return remote(
            mid[c].at[x_far, h], far[c].at[h], r_send.at[c, 1 + h], r_recv.at[c, 1 + h],
            near(3 if h else 1, 0),
        )

    def plain_copy(c, h):
        return remote(
            mid[c].at[x_down if h == 0 else x_up, h], rs2[c].at[1 - h, h],
            r_send.at[c, 3 + h], r_recv.at[c, 3 + h], near(1 if h else 3, 0),
        )

    def added_copy(c, h):
        return remote(
            added[c].at[h], rs2[c].at[h, h], r_send.at[c, 5 + h], r_recv.at[c, 5 + h],
            near(3 if h else 1, 0),
        )

    def to_across(c):
        return remote(wsend[c], rs3[c], r_send.at[c, 7], r_recv.at[c, 7], across)

    def stage_one(c):
        part = lax.dot_general(
            att[...], ofull[STARTS[c] : STARTS[c] + COLS[c], :], (((1,), (1,)), ((), ())),
            preferred_element_type=F32,
        )
        terms[c][...] = part.astype(BF16).reshape(2, 256, COLS[c])
        to_sibling(c).start()

    def stage_two(c):
        to_sibling(c).wait_recv()
        both = (terms[c][core].astype(F32) + rs1[c][...].astype(F32)).astype(BF16)
        both = both.reshape(2, 4, 32, COLS[c])
        for xx in range(4):
            for h in range(2):
                mid[c][xx, h] = both[h, xx]
        for h in range(2):
            far_copy(c, h).start()
        for h in range(2):
            plain_copy(c, h).start()

    def stage_relay(c):
        for h in range(2):
            far_copy(c, h).wait_recv()
            mine_too = mid[c][x_down if h else x_up, h].astype(F32)
            added[c][h] = (mine_too + far[c][h].astype(F32)).astype(BF16)
            added_copy(c, h).start()

    def stage_three(c):
        for h in range(2):
            plain_copy(c, h).wait_recv()
            added_copy(c, h).wait_recv()

        def summed(h):
            s = mid[c][x, h].astype(F32)
            for side in range(2):
                s += rs2[c][side, h].astype(F32)
            return s

        wsend[c][...] = summed(1 - half).astype(BF16)
        to_across(c).start()
        wown[c][...] = summed(half)

    scale = ls_ref[...].reshape(1, D)

    def stage_four(c):
        to_across(c).wait_recv()
        cols = slice(STARTS[c], STARTS[c] + COLS[c])
        projected = wown[c][...] + rs3[c][...].astype(F32)
        out_ref[:, cols] = (
            tok_ref[:, cols].astype(F32) + scale[:, cols] * projected
        ).astype(BF16)

    for t in range(CHUNKS + 3):
        if t < CHUNKS:
            stage_one(t)
        if 0 <= t - 1 < CHUNKS:
            stage_two(t - 1)
        if 0 <= t - 2 < CHUNKS:
            stage_relay(t - 2)
        if 0 <= t - 3 < CHUNKS:
            stage_three(t - 3)
    for k in range(5):
        z8_copy(k).wait_send()
    for slot in range(1, 15):
        for p in range(2):
            tok_copy(half, x, core, p, sibling, slot).wait_send()
    sent(0)
    sent(1)
    for c in range(CHUNKS):
        to_sibling(c).wait_send()
        for h in range(2):
            far_copy(c, h).wait_send()
            plain_copy(c, h).wait_send()
            added_copy(c, h).wait_send()

    for c in range(CHUNKS):
        stage_four(c)

    for c in range(CHUNKS):
        to_across(c).wait_send()


def chunked(dtype, *dims):
    return [pltpu.VMEM((*dims, cols), dtype) for cols in COLS]


def shards(tokens, norm_gain, qkv_weight, q_gain, k_gain, out_weight, layer_scale):
    vmem = pl.BlockSpec(memory_space=pltpu.VMEM)
    dma = pltpu.SemaphoreType.DMA
    return pl.pallas_call(
        kernel,
        out_shape=jax.ShapeDtypeStruct((32, D), BF16),
        in_specs=[vmem] * 7,
        out_specs=vmem,
        scratch_shapes=[
            pltpu.VMEM((512, D), BF16),
            pltpu.VMEM((32, 2, QKV_ROWS, 128), BF16),
            pltpu.VMEM((32, 2, OUT_ROWS, 128), BF16),
            pltpu.VMEM((3, D, 256), BF16),
            pltpu.VMEM((D, 256), BF16),
            pltpu.VMEM((2, 512, 256), F32),
            pltpu.VMEM((3, 512, 256), BF16),
            pltpu.VMEM((512, 256), BF16),
            pltpu.VMEM((128, 512), F32),
            pltpu.VMEM((8, 8, 128), F32),
            pltpu.VMEM((8, 128), F32),
            pltpu.VMEM((8, 128), F32),
            *chunked(BF16, 2, 256),
            *chunked(BF16, 256),
            *chunked(BF16, 4, 2, 32),
            *chunked(BF16, 2, 32),
            *chunked(BF16, 2, 32),
            *chunked(BF16, 2, 2, 32),
            *chunked(F32, 32),
            *chunked(BF16, 32),
            *chunked(BF16, 32),
            dma((16, 2)),
            dma((15, 2)),
            dma((5,)),
            dma((5,)),
            dma((2, 32, 2)),
            dma((2, 6, 8, 2)),
            dma((9,)),
            dma((8,)),
            dma((CHUNKS, 8)),
            dma((CHUNKS, 8)),
        ],
        compiler_params=pltpu.CompilerParams(
            collective_id=0, has_side_effects=True, vmem_limit_bytes=60 * 1024 * 1024
        ),
        cost_estimate=pl.CostEstimate(
            flops=4_000_000_000, bytes_accessed=1_000_000, transcendentals=600_000
        ),
    )(
        tokens, norm_gain, qkv_weight, out_weight.T, q_gain, k_gain, layer_scale
    )


def solution(mesh):
    placed = (
        P(("dp", "tensor"), None),
        P(),
        P(None, "dp", "tensor"),
        P("tensor"),
        P("tensor"),
        P("tensor", "dp"),
        P(),
    )
    return jax.shard_map(
        shards, mesh=mesh, in_specs=placed, out_specs=P(("dp", "tensor"), None), check_vma=False
    )
```

```python
import jax
import jax.numpy as jnp
from jax import lax
from jax.experimental import pallas as pl
from jax.experimental.pallas import tpu as pltpu
from jax.sharding import PartitionSpec as P

D = 3200
HEADS = 25
HD = 128
EPS = 1e-06
WIDTH = HEADS * HD
QKV_ROWS = 304
OUT_ROWS = 112
COLS = (512, 640, 768, 768, 512)
CHUNKS = len(COLS)
STARTS = tuple(sum(COLS[:c]) for c in range(CHUNKS))
MESH = pl.DeviceIdType.MESH
F32 = jnp.float32
BF16 = jnp.bfloat16


def device(y, z, half, x, core):
    return (z * 4 + y, half * 8 + x * 2 + core)


def kernel(*refs):
    tok_ref, gain_ref, qkv_ref, o_ref, qg_ref, kg_ref, ls_ref, out_ref = refs[:8]
    xg, abuf, bbuf, wfull, ofull, qkf, heads, att, stage, srecv, szrecv, sown = refs[8:20]
    chunk_refs = refs[20:-10]
    terms, rs1, mid, far, added, rs2, wown, wsend, rs3 = [
        chunk_refs[i * CHUNKS : (i + 1) * CHUNKS] for i in range(9)
    ]
    tok_recv, tok_send, z8_recv, z8_send, w_recv, w_send = refs[-10:-4]
    s_recv, s_send, r_recv, r_send = refs[-4:]
    dp = lax.axis_index("dp")
    tensor = lax.axis_index("tensor")
    y, z = dp % 4, dp // 4
    half, x, core = tensor // 8, (tensor // 2) % 4, tensor % 2
    y_up, y_down, y_far = (y + 1) % 4, (y + 3) % 4, (y + 2) % 4
    sibling = device(y, z, half, x, 1 - core)
    across = device(y, z, 1 - half, x, core)

    def near(dx, other):
        c = (core + other) % 2
        return device(y, z, half, (x + dx) % 4, c)

    barrier = pltpu.get_barrier_semaphore()

    def greet(target):
        pl.semaphore_signal(barrier, 1, device_id=target, device_id_type=MESH)

    greet(across)
    greet(device(y_up, z, half, x, core))
    greet(device(y_down, z, half, x, core))
    for dx in range(4):
        for other in range(2):
            if dx or other:
                greet(near(dx, other))

    @pl.when(z > 0)
    def _():
        greet(device(y, z - 1, half, x, core))

    @pl.when(z < 7)
    def _():
        greet(device(y, z + 1, half, x, core))

    def remote(src, dst, send, recv, target):
        return pltpu.make_async_remote_copy(
            src_ref=src, dst_ref=dst, send_sem=send, recv_sem=recv,
            device_id=target, device_id_type=MESH,
        )

    def arrived(ref, sem):
        pltpu.make_async_copy(ref, ref, sem).wait()

    def row_block(h, xx, c, p):
        return pl.ds(pl.multiple_of(c * 256 + h * 128 + xx * 32 + p * 16, 16), 16)

    tok = tok_ref[...].astype(F32)
    sq = jnp.sum(tok * tok, axis=1, keepdims=True)
    normed = (
        tok * lax.rsqrt(sq / D + EPS) * gain_ref[...].astype(F32).reshape(1, D)
    ).astype(BF16)
    for p in range(2):
        xg[row_block(half, x, core, p), :] = normed[p * 16 : p * 16 + 16, :]
    mine = z * 4 + y
    for p in range(2):
        cols = slice(p * 128, p * 128 + 128)
        abuf[mine, p] = jnp.concatenate(
            [qkv_ref[i, :, cols] for i in range(3)]
            + [jnp.zeros((QKV_ROWS - 300, 128), BF16)],
            axis=0,
        )
    for p in range(2):
        bbuf[mine, p] = jnp.concatenate(
            [
                o_ref[:, p * 128 : p * 128 + 128],
                jnp.zeros((OUT_ROWS - 100, 128), BF16),
            ],
            axis=0,
        )

    pl.semaphore_wait(
        barrier, 10 + (z > 0).astype(jnp.int32) + (z < 7).astype(jnp.int32)
    )

    def tok_copy(h, xx, c, p, target, slot):
        ref = xg.at[row_block(h, xx, c, p), :]
        return remote(
            ref, ref, tok_send.at[slot, p], tok_recv.at[h * 8 + xx * 2 + c, p], target
        )

    def tok_wait(h, xx, c, p):
        arrived(xg.at[row_block(h, xx, c, p), :], tok_recv.at[h * 8 + xx * 2 + c, p])

    def tok_spread(h, p, base):
        for dx in (2, 1, 3):
            tok_copy(h, x, core, p, near(dx, 0), base + dx - 1).start()
        tok_copy(h, x, core, p, sibling, base + 3).start()

    def tok_pass(h, p, base):
        for dx in (1, 3, 2):
            xx = (x + dx) % 4
            tok_wait(h, xx, core, p)
            tok_copy(h, xx, core, p, sibling, base + dx - 1).start()


    def z8_copy(k):
        ref = xg.at[pl.ds(pl.multiple_of(core * 256 + half * 128 + x * 32, 32), 32), pl.ds(k * 640, 640)]
        return remote(ref, ref, z8_send.at[k], z8_recv.at[k], across)

    def z8_wait(k):
        ref = xg.at[pl.ds(pl.multiple_of(core * 256 + (1 - half) * 128 + x * 32, 32), 32), pl.ds(k * 640, 640)]
        arrived(ref, z8_recv.at[k])

    bufs = (abuf, bbuf)

    def w_copy(cls, zs, yy, part, kind, target):
        b = zs * 4 + yy
        ref = bufs[cls].at[b, part]
        return remote(
            ref, ref, w_send.at[cls, kind, zs, part], w_recv.at[cls, b, part], target
        )

    def w_wait(cls, zs, yy, part):
        b = zs * 4 + yy
        arrived(bufs[cls].at[b, part], w_recv.at[cls, b, part])

    def z_right(cls, zs, part):
        return w_copy(cls, zs, y, part, 0, device(y, z + 1, half, x, core))

    def z_left(cls, zs, part):
        return w_copy(cls, zs, y, part, 1, device(y, z - 1, half, x, core))

    def y_plus(cls, zs, part):
        return w_copy(cls, zs, y, part, 2, device(y_up, z, half, x, core))

    def y_minus(cls, zs, part):
        return w_copy(cls, zs, y, part, 3, device(y_down, z, half, x, core))

    def pass_plus(cls, zs):
        return w_copy(cls, zs, y_down, 0, 4, device(y_up, z, half, x, core))

    def pass_minus(cls, zs):
        return w_copy(cls, zs, y_up, 1, 5, device(y_down, z, half, x, core))

    def send_y(cls, zs):
        y_plus(cls, zs, 0).start()
        y_minus(cls, zs, 1).start()
        y_plus(cls, zs, 1).start()
        y_minus(cls, zs, 0).start()

    def first_step(cls, spread):
        for part in range(2):

            @pl.when(z < 7)
            def _():
                z_right(cls, z, part).start()

            @pl.when(z > 0)
            def _():
                z_left(cls, z, part).start()

        if spread:
            send_y(cls, z)

    def step(cls, s, spread):
        for part in range(2):

            @pl.when(z >= s)
            def _():
                w_wait(cls, z - s, y, part)

                @pl.when(z < 7)
                def _():
                    z_right(cls, z - s, part).start()

            @pl.when(z + s <= 7)
            def _():
                w_wait(cls, z + s, y, part)

                @pl.when(z > 0)
                def _():
                    z_left(cls, z + s, part).start()

        if spread:

            @pl.when(z >= s)
            def _():
                send_y(cls, z - s)

            @pl.when(z + s <= 7)
            def _():
                send_y(cls, z + s)

    def pass_one(cls, zs):
        w_wait(cls, zs, y_down, 0)
        pass_plus(cls, zs).start()
        w_wait(cls, zs, y_up, 1)
        pass_minus(cls, zs).start()

    def passes(cls, s):
        @pl.when(z >= s)
        def _():
            pass_one(cls, z - s)

        @pl.when((z + s <= 7) & (s > 0))
        def _():
            pass_one(cls, z + s)

    def finish(cls, zs):
        w_wait(cls, zs, y_down, 1)
        w_wait(cls, zs, y_up, 0)
        for part in range(2):
            w_wait(cls, zs, y_far, part)

    def sent(cls):
        @pl.loop(0, 8)
        def _(zs):
            for part in range(2):

                @pl.when((z < 7) & (zs <= z))
                def _():
                    z_right(cls, zs, part).wait_send()

                @pl.when((z > 0) & (zs >= z))
                def _():
                    z_left(cls, zs, part).wait_send()

                y_plus(cls, zs, part).wait_send()
                y_minus(cls, zs, part).wait_send()
            pass_plus(cls, zs).wait_send()
            pass_minus(cls, zs).wait_send()

    first_step(0, True)
    for p in range(2):
        tok_spread(half, p, 1)
    z8_copy(0).start()
    step(0, 1, True)
    z8_copy(1).start()
    step(0, 2, True)
    z8_copy(2).start()
    passes(0, 0)
    step(0, 3, True)
    z8_copy(3).start()
    passes(0, 1)
    for p in range(2):
        tok_pass(half, p, 5)
    step(0, 4, True)
    z8_copy(4).start()
    first_step(1, False)
    passes(0, 2)
    step(0, 5, True)
    step(1, 1, False)
    passes(0, 3)
    step(0, 6, True)
    step(1, 2, False)
    for k in range(5):
        z8_wait(k)
    for p in range(2):
        tok_spread(1 - half, p, 8)
    passes(0, 4)
    step(0, 7, True)
    step(1, 3, False)
    passes(0, 5)
    step(1, 4, False)
    passes(0, 6)
    step(1, 5, False)
    passes(0, 7)
    step(1, 6, False)
    tok_pass(1 - half, 0, 12)
    tok_pass(1 - half, 1, 12)
    step(1, 7, False)
    @pl.loop(0, 8)
    def _(s):
        @pl.when(z >= s)
        def _():
            send_y(1, z - s)

        @pl.when((z + s <= 7) & (s > 0))
        def _():
            send_y(1, z + s)


    @pl.loop(0, 8)
    def _(zs):
        finish(0, zs)
        rows = pl.ds(pl.multiple_of(zs * 400, 16), 400)
        for i in range(3):
            for p in range(2):
                wfull[i, rows, p * 128 : p * 128 + 128] = jnp.concatenate(
                    [abuf[zs * 4 + j, p, i * 100 : i * 100 + 100, :] for j in range(4)],
                    axis=0,
                )

    for h in range(2):
        for xx in range(4):
            for p in range(2):
                tok_wait(h, xx, 1 - core, p)

    keep = (
        tensor * 2 + lax.broadcasted_iota(jnp.int32, (1, 256), 1) // HD < HEADS
    ).astype(F32)

    def project(i):
        return jnp.dot(xg[...], wfull[i], preferred_element_type=F32) * keep

    sums = []
    for i in range(2):
        qkf[i] = project(i)
        sums.append(jnp.sum(qkf[i] * qkf[i], axis=1, keepdims=True))
    lane = lax.broadcasted_iota(jnp.int32, (512, 128), 1)
    stage[...] = jnp.where(
        lane == 0, sums[0], jnp.where(lane == 1, sums[1], 0.0)
    ).T
    spot = x * 2 + core
    for i in range(2):
        for j in range(4):
            srecv[spot, pl.ds(i * 4 + j, 1), :] = stage[i : i + 1, j * 128 : j * 128 + 128]

    def sum_copy(dx, other):
        return remote(
            srecv.at[spot], srecv.at[spot], s_send.at[dx * 2 + other],
            s_recv.at[spot], near(dx, other),
        )

    for dx in range(4):
        for other in range(2):
            if dx or other:
                sum_copy(dx, other).start()

    heads[2] = project(2).astype(BF16)

    @pl.loop(0, 4)
    def _(s):
        passes(1, s)

    for dx in range(4):
        for other in range(2):
            if dx or other:
                other_spot = ((x + dx) % 4) * 2 + (core + other) % 2
                arrived(srecv.at[other_spot], s_recv.at[other_spot])
    total = srecv[0]
    for i in range(1, 8):
        total += srecv[i]
    sown[...] = total
    across_sum = remote(sown, szrecv, s_send.at[0], s_recv.at[8], across)
    for dx in range(4):
        for other in range(2):
            if dx or other:
                sum_copy(dx, other).wait_send()
    across_sum.start()

    @pl.loop(4, 8)
    def _(s):
        passes(1, s)

    across_sum.wait()
    total = sown[...] + szrecv[...]
    for i in range(2):
        for j in range(4):
            stage[i : i + 1, j * 128 : j * 128 + 128] = total[i * 4 + j : i * 4 + j + 1, :]
    columns = stage[...].T
    heads[0] = (
        qkf[0] * lax.rsqrt(columns[:, 0:1] / WIDTH + EPS) * qg_ref[...].reshape(1, 256)
    ).astype(BF16)
    heads[1] = (
        qkf[1] * lax.rsqrt(columns[:, 1:2] / WIDTH + EPS) * kg_ref[...].reshape(1, 256)
    ).astype(BF16)

    for h in range(2):
        cols = slice(h * HD, h * HD + HD)

        @pl.loop(0, 2)
        def _(r):
            rows = pl.ds(pl.multiple_of(r * 256, 256), 256)
            scores = lax.dot_general(
                heads[0, rows, cols], heads[1, :, cols], (((1,), (1,)), ((), ())),
                preferred_element_type=F32,
            ) * HD ** (-0.5)
            e = jnp.exp(scores - jnp.max(scores, axis=1, keepdims=True))
            probs = (e / jnp.sum(e, axis=1, keepdims=True)).astype(BF16)
            att[rows, cols] = jnp.dot(
                probs, heads[2, :, cols], preferred_element_type=F32
            ).astype(BF16)

    @pl.loop(0, 8)
    def _(zs):
        finish(1, zs)
        rows = pl.ds(pl.multiple_of(zs * 400, 16), 400)
        for p in range(2):
            ofull[rows, p * 128 : p * 128 + 128] = jnp.concatenate(
                [bbuf[zs * 4 + j, p, 0:100, :] for j in range(4)], axis=0
            )

    x_up, x_down, x_far = (x + 1) % 4, (x + 3) % 4, (x + 2) % 4

    def to_sibling(c):
        return remote(
            terms[c].at[1 - core], rs1[c], r_send.at[c, 0], r_recv.at[c, 0], sibling
        )

    def far_copy(c, h):
        return remote(
            mid[c].at[x_far, h], far[c].at[h], r_send.at[c, 1 + h], r_recv.at[c, 1 + h],
            near(3 if h else 1, 0),
        )

    def plain_copy(c, h):
        return remote(
            mid[c].at[x_down if h == 0 else x_up, h], rs2[c].at[1 - h, h],
            r_send.at[c, 3 + h], r_recv.at[c, 3 + h], near(1 if h else 3, 0),
        )

    def added_copy(c, h):
        return remote(
            added[c].at[h], rs2[c].at[h, h], r_send.at[c, 5 + h], r_recv.at[c, 5 + h],
            near(3 if h else 1, 0),
        )

    def to_across(c):
        return remote(wsend[c], rs3[c], r_send.at[c, 7], r_recv.at[c, 7], across)

    def stage_one(c):
        part = lax.dot_general(
            att[...], ofull[STARTS[c] : STARTS[c] + COLS[c], :], (((1,), (1,)), ((), ())),
            preferred_element_type=F32,
        )
        terms[c][...] = part.astype(BF16).reshape(2, 256, COLS[c])
        to_sibling(c).start()

    def stage_two(c):
        to_sibling(c).wait_recv()
        both = (terms[c][core].astype(F32) + rs1[c][...].astype(F32)).astype(BF16)
        both = both.reshape(2, 4, 32, COLS[c])
        for xx in range(4):
            for h in range(2):
                mid[c][xx, h] = both[h, xx]
        for h in range(2):
            far_copy(c, h).start()
        for h in range(2):
            plain_copy(c, h).start()

    def stage_relay(c):
        for h in range(2):
            far_copy(c, h).wait_recv()
            mine_too = mid[c][x_down if h else x_up, h].astype(F32)
            added[c][h] = (mine_too + far[c][h].astype(F32)).astype(BF16)
            added_copy(c, h).start()

    def stage_three(c):
        for h in range(2):
            plain_copy(c, h).wait_recv()
            added_copy(c, h).wait_recv()

        def summed(h):
            s = mid[c][x, h].astype(F32)
            for side in range(2):
                s += rs2[c][side, h].astype(F32)
            return s

        wsend[c][...] = summed(1 - half).astype(BF16)
        to_across(c).start()
        wown[c][...] = summed(half)

    scale = ls_ref[...].reshape(1, D)

    def stage_four(c):
        to_across(c).wait_recv()
        cols = slice(STARTS[c], STARTS[c] + COLS[c])
        projected = wown[c][...] + rs3[c][...].astype(F32)
        out_ref[:, cols] = (
            tok_ref[:, cols].astype(F32) + scale[:, cols] * projected
        ).astype(BF16)

    for t in range(CHUNKS + 3):
        if t < CHUNKS:
            stage_one(t)
        if 0 <= t - 1 < CHUNKS:
            stage_two(t - 1)
        if 0 <= t - 2 < CHUNKS:
            stage_relay(t - 2)
        if 0 <= t - 3 < CHUNKS:
            stage_three(t - 3)
    for k in range(5):
        z8_copy(k).wait_send()
    for slot in range(1, 15):
        for p in range(2):
            tok_copy(half, x, core, p, sibling, slot).wait_send()
    sent(0)
    sent(1)
    for c in range(CHUNKS):
        to_sibling(c).wait_send()
        for h in range(2):
            far_copy(c, h).wait_send()
            plain_copy(c, h).wait_send()
            added_copy(c, h).wait_send()

    for c in range(CHUNKS):
        stage_four(c)

    for c in range(CHUNKS):
        to_across(c).wait_send()


def chunked(dtype, *dims):
    return [pltpu.VMEM((*dims, cols), dtype) for cols in COLS]


def shards(tokens, norm_gain, qkv_weight, q_gain, k_gain, out_weight, layer_scale):
    vmem = pl.BlockSpec(memory_space=pltpu.VMEM)
    dma = pltpu.SemaphoreType.DMA
    return pl.pallas_call(
        kernel,
        out_shape=jax.ShapeDtypeStruct((32, D), BF16),
        in_specs=[vmem] * 7,
        out_specs=vmem,
        scratch_shapes=[
            pltpu.VMEM((512, D), BF16),
            pltpu.VMEM((32, 2, QKV_ROWS, 128), BF16),
            pltpu.VMEM((32, 2, OUT_ROWS, 128), BF16),
            pltpu.VMEM((3, D, 256), BF16),
            pltpu.VMEM((D, 256), BF16),
            pltpu.VMEM((2, 512, 256), F32),
            pltpu.VMEM((3, 512, 256), BF16),
            pltpu.VMEM((512, 256), BF16),
            pltpu.VMEM((128, 512), F32),
            pltpu.VMEM((8, 8, 128), F32),
            pltpu.VMEM((8, 128), F32),
            pltpu.VMEM((8, 128), F32),
            *chunked(BF16, 2, 256),
            *chunked(BF16, 256),
            *chunked(BF16, 4, 2, 32),
            *chunked(BF16, 2, 32),
            *chunked(BF16, 2, 32),
            *chunked(BF16, 2, 2, 32),
            *chunked(F32, 32),
            *chunked(BF16, 32),
            *chunked(BF16, 32),
            dma((16, 2)),
            dma((15, 2)),
            dma((5,)),
            dma((5,)),
            dma((2, 32, 2)),
            dma((2, 6, 8, 2)),
            dma((9,)),
            dma((8,)),
            dma((CHUNKS, 8)),
            dma((CHUNKS, 8)),
        ],
        compiler_params=pltpu.CompilerParams(
            collective_id=0, has_side_effects=True, vmem_limit_bytes=60 * 1024 * 1024
        ),
        cost_estimate=pl.CostEstimate(
            flops=4_000_000_000, bytes_accessed=1_000_000, transcendentals=600_000
        ),
    )(
        tokens, norm_gain, qkv_weight, out_weight.T, q_gain, k_gain, layer_scale
    )


def solution(mesh):
    placed = (
        P(("dp", "tensor"), None),
        P(),
        P(None, "dp", "tensor"),
        P("tensor"),
        P("tensor"),
        P("tensor", "dp"),
        P(),
    )
    return jax.shard_map(
        shards, mesh=mesh, in_specs=placed, out_specs=P(("dp", "tensor"), None), check_vma=False
    )
```
